128 devices in a mesh: pipe: 2 (over core), ctx: 16 (over y, x), tp: 4 (over z).
Axes of the slice: x: 4, y: 4, z: 4, core: 2. Of those that a mesh axis runs over, the one named last changes fastest.
Arguments:
- queries: bfloat16 [2, 8192, 3584], P('pipe', ('ctx', 'tp')), may hold values from -20 to 20
- keys: bfloat16 [2, 8192, 3584], P('pipe', ('ctx', 'tp')), may hold values from -6 to 6
- values: bfloat16 [2, 8192, 3584], P('pipe', ('ctx', 'tp')), may hold values from -6 to 6
- out_grad: bfloat16 [2, 8192, 3584], P('pipe', ('ctx', 'tp')), may hold values from -6 to 6
- chosen: int32 [2, 16, 3], P('pipe'), may hold values from 0 to 14, as said below
Outputs:
- out_next: bfloat16 [2, 8192, 3584], P('pipe', ('ctx', 'tp'))
- query_back: bfloat16 [2, 8192, 3584], P('pipe', ('ctx', 'tp'))
- key_back: bfloat16 [2, 8192, 3584], P('pipe', ('ctx', 'tp'))
- value_back: bfloat16 [2, 8192, 3584], P('pipe', ('ctx', 'tp'))
The draws below stay inside these ranges and needn't reach their ends.
Inputs may be any that keep to these rules, and one draw needn't show every extreme that they name: chosen[s, i, j] is at most i; its entries below i are distinct, there are min(i, 3) of them and the others equal i; block i - 1 is always among them; earlier blocks are chosen more often.
All inputs are finite; a program needn't handle non-finite values.
Results may differ from the reference program's by a relative error of at most 0.0056.
Values may be sent and summed in bfloat16 or wider, within the bound.
No kernel may reach another device: no remote copies, remote signals or barrier semaphores. Data moves between devices by JAX's collectives and lax.ppermute only.
A program may use at most 384 MiB of HBM per device.

```python
import math
import jax
import jax.numpy as jnp
from jax import lax

HEADS = 28
HD = 128
BLK = 512
TOPK = 3
SEGMENTS = 2
NB = 16
SEQ = 8192
HF = 3584


def draw_queries(key, part):
    key = jax.random.fold_in(key, 11)
    result = jnp.clip(jax.random.normal(key, (SEGMENTS, SEQ, HF), jnp.float32), -6.0, 6.0)
    return result.astype(jnp.bfloat16)


def draw_keys(key, part):
    key = jax.random.fold_in(key, 12)
    result = jnp.clip(jax.random.normal(key, (SEGMENTS, SEQ, HF), jnp.float32), -6.0, 6.0)
    return result.astype(jnp.bfloat16)


def draw_chosen(key, part):
    key = jax.random.fold_in(key, 5)
    noise = jax.random.randint(key, (SEGMENTS, NB, NB), 0, NB)
    row = jnp.arange(NB, dtype=jnp.int32)[:, None]
    col = jnp.arange(NB, dtype=jnp.int32)[None, :]
    score = (noise + NB - col) * (2 * NB) + (NB - col)
    score = jnp.where(col == row - 1, 8 * NB * NB, score)
    score = jnp.where(col >= row, -1 - col, score)
    picked = lax.top_k(score, TOPK)[1].astype(jnp.int32)
    return jnp.where(picked >= row, row, picked).astype(jnp.int32)


def block_levels(rng, shape, split, low, high):
    gain = 1.0
    for axis_at, blocks in split:
        draws = jax.random.uniform(jax.random.fold_in(jax.random.fold_in(rng, 6), axis_at), (blocks,), jnp.float32, low / len(split), high / len(split))
        gain = gain * jnp.repeat(jnp.exp(draws), shape[axis_at] // blocks).reshape((-1,) + (1,) * (len(shape) - 1 - axis_at))
    return gain


def scatter_about(rng, shape, scale, bound, split=(), kind=jnp.bfloat16):
    loudness = block_levels(rng, shape, split, -0.22, 0.18) if split else 1.0
    values = jax.random.normal(rng, shape, jnp.float32) * scale * loudness
    return jnp.minimum(jnp.maximum(values, -bound), bound).astype(kind)


def setup_inputs(seed: int = 0) -> dict:
    seeds = jax.random.split(jax.random.key(seed), 6)
    return {
        "queries": draw_queries(jax.random.fold_in(seeds[5], 71), 0),
        "keys": draw_keys(jax.random.fold_in(seeds[5], 71), 0),
        "values": scatter_about(seeds[2], (SEGMENTS, SEQ, HF), 1.0, 6.0, ((0, 2), (1, 64))),
        "out_grad": scatter_about(seeds[3], (SEGMENTS, SEQ, HF), 1.0, 6.0, ((0, 2), (1, 64))),
        "chosen": draw_chosen(jax.random.fold_in(seeds[5], 71), 0),
    }


def slot_mask(picked, block, size, count):
    rows = lax.broadcasted_iota(jnp.int32, (size, size), 0)
    cols = lax.broadcasted_iota(jnp.int32, (size, size), 1)
    parts = [jnp.broadcast_to(picked[j] < block, (size, size)) for j in range(count)]
    parts.append(cols <= rows)
    return jnp.concatenate(parts, axis=1)

def widen(array):
    return array.astype(jnp.float32)

def head_forward(query, keyset, valueset, valid):
    scale = 1.0 / math.sqrt(query.shape[-1])
    scores = jnp.dot(widen(query), widen(keyset).T, preferred_element_type=jnp.float32) * scale
    scores = jnp.where(valid, scores, -jnp.inf)
    top = lax.optimization_barrier(jnp.max(scores, axis=-1, keepdims=True))
    total = jnp.log(lax.optimization_barrier(jnp.sum(jnp.exp(scores - top), axis=-1, keepdims=True))) + top
    probs = lax.optimization_barrier(jnp.exp(scores - total).astype(jnp.bfloat16))
    attended = jnp.dot(widen(probs), widen(valueset), preferred_element_type=jnp.float32).astype(jnp.bfloat16)
    return (attended, total)

def head_backward(query, keyset, valueset, grad, attended, total, valid):
    scale = 1.0 / math.sqrt(query.shape[-1])
    scores = jnp.dot(widen(query), widen(keyset).T, preferred_element_type=jnp.float32) * scale
    scores = jnp.where(valid, scores, -jnp.inf)
    probs = jnp.exp(scores - total)
    low = lax.optimization_barrier(probs.astype(jnp.bfloat16))
    value_part = jnp.dot(widen(low).T, widen(grad), preferred_element_type=jnp.float32)
    prob_grad = jnp.dot(widen(grad), widen(valueset).T, preferred_element_type=jnp.float32)
    delta = lax.optimization_barrier(jnp.sum(widen(grad) * widen(attended), axis=-1, keepdims=True))
    score_grad = lax.optimization_barrier((probs * (prob_grad - delta)).astype(jnp.bfloat16))
    query_part = (jnp.dot(widen(score_grad), widen(keyset), preferred_element_type=jnp.float32) * scale).astype(jnp.bfloat16)
    key_part = jnp.dot(widen(score_grad).T, widen(query), preferred_element_type=jnp.float32) * scale
    return (query_part, key_part, value_part)

def one_segment(items):
    query_all, key_all, value_all, grad_all, picks = items
    count = picks.shape[0]
    qblk = query_all.reshape(count, BLK, HEADS, HD)
    kblk = key_all.reshape(count, BLK, HEADS, HD)
    vblk = value_all.reshape(count, BLK, HEADS, HD)
    gblk = grad_all.reshape(count, BLK, HEADS, HD)

    def step(carry, index):
        key_acc, value_acc = carry
        picked = picks[index]
        blocks = jnp.concatenate([picked, index[None]]).astype(jnp.int32)
        valid = slot_mask(picked, index, BLK, TOPK)
        keyset = kblk[blocks].reshape((TOPK + 1) * BLK, HEADS, HD)
        valueset = vblk[blocks].reshape((TOPK + 1) * BLK, HEADS, HD)
        query = qblk[index]
        grad = gblk[index]
        attended, total = jax.vmap(head_forward, in_axes=(1, 1, 1, None), out_axes=(1, 1))(query, keyset, valueset, valid)
        query_part, key_part, value_part = jax.vmap(head_backward, in_axes=(1, 1, 1, 1, 1, 1, None), out_axes=(1, 1, 1))(query, keyset, valueset, grad, attended, total, valid)
        key_acc = key_acc.at[blocks].add(key_part.reshape(TOPK + 1, BLK, HEADS, HD))
        value_acc = value_acc.at[blocks].add(value_part.reshape(TOPK + 1, BLK, HEADS, HD))
        return ((key_acc, value_acc), (attended, query_part))
    empty = jnp.zeros((count, BLK, HEADS, HD), jnp.float32)
    indices = jnp.arange(count, dtype=jnp.int32)
    (key_acc, value_acc), (attended, query_part) = lax.scan(step, (empty, empty), indices)
    width = HEADS * HD
    return (attended.reshape(count * BLK, width), query_part.reshape(count * BLK, width), key_acc.astype(jnp.bfloat16).reshape(count * BLK, width), value_acc.astype(jnp.bfloat16).reshape(count * BLK, width))

def reference(queries, keys, values, out_grad, chosen):
    attended, query_grad, key_grad, value_grad = lax.map(one_segment, (queries, keys, values, out_grad, chosen))
    out_next = jnp.concatenate([jnp.zeros_like(attended[:1]), attended[:-1]], axis=0)
    query_back = jnp.concatenate([query_grad[1:], jnp.zeros_like(query_grad[:1])], axis=0)
    key_back = jnp.concatenate([key_grad[1:], jnp.zeros_like(key_grad[:1])], axis=0)
    value_back = jnp.concatenate([value_grad[1:], jnp.zeros_like(value_grad[:1])], axis=0)
    return (out_next, query_back, key_back, value_back)
```

```python
import math

import jax
import jax.numpy as jnp
from jax import lax
from jax.experimental import pallas as pl
from jax.experimental.pallas import tpu as pltpu
from jax.sharding import PartitionSpec as P

HD = 128
BLK = 512
TOPK = 3
HALF = 64
PART = 4
ROWS = PART * HALF
WIDE = 32
STEP = 4
VMEM = 56 * 1024 * 1024

BF = jnp.bfloat16
F32 = jnp.float32


def dot(a, b, dims):
    return lax.dot_general(a, b, (dims, ((), ())), preferred_element_type=F32)


NN = ((1,), (0,))


def spread_kernel(k_ref, v_ref, q_ref, g_ref, out_ref):
    for a, ref in enumerate((k_ref, v_ref, q_ref, g_ref)):
        for h in range(STEP):
            for half in range(2):
                out_ref[half, h, a] = ref[0, half * HALF : (half + 1) * HALF, h * HD : (h + 1) * HD]


def spread(keys, values, queries, grads):
    heads = keys.shape[2] // HD
    item = pl.BlockSpec((1, 2 * HALF, STEP * HD), lambda i: (0, 0, i))
    return pl.pallas_call(
        spread_kernel,
        grid=(heads // STEP,),
        in_specs=[item] * 4,
        out_specs=pl.BlockSpec((2, STEP, 4, HALF, HD), lambda i: (0, i, 0, 0, 0)),
        out_shape=jax.ShapeDtypeStruct((2, WIDE, 4, HALF, HD), BF),
        compiler_params=pltpu.CompilerParams(vmem_limit_bytes=VMEM),
        name="spread_heads",
    )(keys, values, queries, grads)


def attend_kernel(
    place_ref, picks_ref, own_ref, other_ref,
    first_ref, mine_ref, theirs_ref,
    kt_ref, vt_ref, s_ref, sum_ref,
):
    nb = picks_ref.shape[0]
    core, seg = place_ref[0], place_ref[1]
    scale = 1.0 / math.sqrt(HD)
    power = scale * math.log2(math.e)

    def part(a, half, b):
        ref = own_ref if half == 0 else other_ref
        return ref[pl.ds(b * PART, PART), a].reshape(ROWS, HD)

    def turn(b, carry):
        for half in range(2):
            kt_ref[half * nb + b] = part(0, half, b).T
            vt_ref[half * nb + b] = part(1, half, b).T
        for a in range(2):
            mine_ref[a, pl.ds(b * PART, PART)] = jnp.zeros((PART, HALF, HD), F32)
            sum_ref[a, pl.ds(b * PART, PART)] = jnp.zeros((PART, HALF, HD), F32)
        return carry

    lax.fori_loop(0, nb, turn, 0)

    def one_block(i, carry):
        q = part(2, 0, i)
        g = part(3, 0, i)
        qt = q.T
        gt = g.T
        slots = [picks_ref[i, j] for j in range(TOPK)] + [i]
        chunks = [(j, half) for j in range(TOPK + 1) for half in range(2)]
        key_at = lax.broadcasted_iota(jnp.int32, (ROWS, ROWS), 0)
        query_at = lax.broadcasted_iota(jnp.int32, (ROWS, ROWS), 1)
        top = jnp.full((1, ROWS), -jnp.inf, F32)
        for n, (j, half) in enumerate(chunks):
            s = dot(part(0, half, slots[j]), qt, NN)
            if j < TOPK:
                valid = slots[j] < i
            elif half == 0:
                valid = key_at <= query_at
            else:
                valid = key_at // HALF < query_at // HALF + core
            s = jnp.where(valid, s, -jnp.inf)
            s_ref[n] = s
            top = jnp.maximum(top, jnp.max(s, axis=0, keepdims=True))
        total = jnp.zeros((1, ROWS), F32)
        for n in range(len(chunks)):
            e = jnp.exp2((s_ref[n] - top) * power)
            s_ref[n] = e
            total = total + jnp.sum(e, axis=0, keepdims=True)
        inverse = 1.0 / total
        out_t = jnp.zeros((HD, ROWS), F32)
        for n, (j, half) in enumerate(chunks):
            p = s_ref[n] * inverse
            low = p.astype(BF)
            s_ref[n] = p
            out_t = out_t + dot(vt_ref[half * nb + slots[j]], low, NN)
            at = pl.ds(slots[j] * PART, PART)
            acc = mine_ref if half == 0 else sum_ref
            acc[1, at] += dot(low, g, NN).reshape(PART, HALF, HD)
        out = out_t.T.astype(BF)
        delta = jnp.sum(gt.astype(F32) * out_t.astype(BF).astype(F32), axis=0, keepdims=True)
        query_t = jnp.zeros((HD, ROWS), F32)
        for n, (j, half) in enumerate(chunks):
            dp = dot(part(1, half, slots[j]), gt, NN)
            ds = (s_ref[n] * (dp - delta)).astype(BF)
            query_t = query_t + dot(kt_ref[half * nb + slots[j]], ds, NN)
            at = pl.ds(slots[j] * PART, PART)
            acc = mine_ref if half == 0 else sum_ref
            acc[0, at] += dot(ds, q, NN).reshape(PART, HALF, HD)
        query = (query_t * scale).T.astype(BF)
        first = jnp.where(seg == 0, out.astype(F32), query.astype(F32)).astype(BF)
        first_ref[pl.ds(i * PART, PART)] = first.reshape(PART, HALF, HD)
        return carry

    lax.fori_loop(0, nb, one_block, 0)

    def finish(b, carry):
        for a in range(2):
            at = pl.ds(b * PART, PART)
            theirs_ref[a, at] = sum_ref[a, at].astype(theirs_ref.dtype)
        return carry

    lax.fori_loop(0, nb, finish, 0)


def attend(place, picks, own, other):
    nb = picks.shape[0]
    n = nb * PART
    smem = pl.BlockSpec(memory_space=pltpu.SMEM)
    vmem = pl.BlockSpec(memory_space=pltpu.VMEM)
    work = 6 * 2 * nb * ROWS * (TOPK + 1) * BLK * HD
    return pl.pallas_call(
        attend_kernel,
        in_specs=[smem, smem, vmem, vmem],
        out_specs=[vmem, vmem, vmem],
        out_shape=[
            jax.ShapeDtypeStruct((n, HALF, HD), BF),
            jax.ShapeDtypeStruct((2, n, HALF, HD), F32),
            jax.ShapeDtypeStruct((2, n, HALF, HD), BF),
        ],
        scratch_shapes=[
            pltpu.VMEM((2 * nb, HD, ROWS), BF),
            pltpu.VMEM((2 * nb, HD, ROWS), BF),
            pltpu.VMEM((2 * (TOPK + 1), ROWS, ROWS), F32),
            pltpu.VMEM((2, n, HALF, HD), F32),
        ],
        compiler_params=pltpu.CompilerParams(vmem_limit_bytes=VMEM),
        cost_estimate=pl.CostEstimate(flops=work, bytes_accessed=20 << 20, transcendentals=0),
        name="attend_head",
    )(place, picks, own, other)


def combine_kernel(first_ref, mine_ref, got_ref, out_ref):
    scale = 1.0 / math.sqrt(HD)
    out_ref[:, 0] = first_ref[...]
    out_ref[:, 1] = ((mine_ref[0] + got_ref[0].astype(F32)) * scale).astype(BF)
    out_ref[:, 2] = (mine_ref[1] + got_ref[1].astype(F32)).astype(BF)


def combine(first, mine, got):
    n = first.shape[0]
    size = n // 4
    return pl.pallas_call(
        combine_kernel,
        grid=(4,),
        in_specs=[
            pl.BlockSpec((size, HALF, HD), lambda i: (i, 0, 0)),
            pl.BlockSpec((2, size, HALF, HD), lambda i: (0, i, 0, 0)),
            pl.BlockSpec((2, size, HALF, HD), lambda i: (0, i, 0, 0)),
        ],
        out_specs=pl.BlockSpec((size, 3, HALF, HD), lambda i: (i, 0, 0, 0)),
        out_shape=jax.ShapeDtypeStruct((n, 3, HALF, HD), BF),
        compiler_params=pltpu.CompilerParams(vmem_limit_bytes=VMEM),
        name="combine_halves",
    )(first, mine, got)


def gather_kernel(place_ref, ao_ref, ag_ref, bo_ref, bg_ref, o_ref, dq_ref, dk_ref, dv_ref):
    core = place_ref[0]

    def fill(ref, own, got, live):
        for h in range(STEP):
            for half in range(2):
                value = jnp.where(core == half, own(h), got(h))
                value = jnp.where(live, value, jnp.zeros_like(value))
                ref[0, half * HALF : (half + 1) * HALF, h * HD : (h + 1) * HD] = value

    fill(o_ref, lambda h: ao_ref[h, 0], lambda h: bo_ref[h], core == 1)
    for a, ref in enumerate((dq_ref, dk_ref, dv_ref)):
        fill(ref, lambda h: ag_ref[h, a], lambda h: bg_ref[h, a], core == 0)


def gather(place, whole, got_out, got_grads, heads):
    item = pl.BlockSpec((1, 2 * HALF, STEP * HD), lambda i: (0, 0, i))
    shape = jax.ShapeDtypeStruct((1, 2 * HALF, heads * HD), BF)
    return pl.pallas_call(
        gather_kernel,
        grid=(heads // STEP,),
        in_specs=[
            pl.BlockSpec(memory_space=pltpu.SMEM),
            pl.BlockSpec((STEP, 1, HALF, HD), lambda i: (i, 0, 0, 0)),
            pl.BlockSpec((STEP, 3, HALF, HD), lambda i: (WIDE // STEP + i, 0, 0, 0)),
            pl.BlockSpec((STEP, HALF, HD), lambda i: (i, 0, 0)),
            pl.BlockSpec((STEP, 3, HALF, HD), lambda i: (i, 0, 0, 0)),
        ],
        out_specs=[item] * 4,
        out_shape=[shape] * 4,
        compiler_params=pltpu.CompilerParams(vmem_limit_bytes=VMEM),
        name="gather_heads",
    )(place, whole, whole, got_out, got_grads)


CHIPS = ("ctx", "tp")
SWAP = [(0, 1), (1, 0)]


def on_device(queries, keys, values, out_grad, chosen):
    heads = queries.shape[2] // HD
    core = lax.axis_index("pipe")
    seg = lax.axis_index(CHIPS) // WIDE
    place = jnp.stack([core, seg]).astype(jnp.int32)
    picks = jnp.where(seg == core, chosen, lax.ppermute(chosen, "pipe", SWAP))[0]

    parts = lax.all_to_all(spread(keys, values, queries, out_grad), "pipe", 0, 0, tiled=True)
    parts = parts.reshape(2 * WIDE, 4, HALF, HD)
    own = lax.all_to_all(parts, CHIPS, 0, 0, tiled=True)
    other = lax.ppermute(own[:, :2], "pipe", SWAP)
    first, mine, theirs = attend(place, picks, own, other)
    whole = combine(first, mine, lax.ppermute(theirs, "pipe", SWAP))

    back = lax.all_to_all(whole, CHIPS, 0, 0, tiled=True)
    got_out = lax.ppermute(back[:heads, 0], "pipe", [(0, 1)])
    got_grads = lax.ppermute(back[WIDE : WIDE + heads], "pipe", [(1, 0)])
    return tuple(gather(place, back, got_out, got_grads, heads))


def solution(mesh):
    placed = P("pipe", CHIPS, None)
    return jax.shard_map(
        on_device,
        mesh=mesh,
        in_specs=(placed,) * 4 + (P("pipe", None, None),),
        out_specs=(placed,) * 4,
        check_vma=False,
    )
```

```python
import math

import jax
import jax.numpy as jnp
from jax import lax
from jax.experimental import pallas as pl
from jax.experimental.pallas import tpu as pltpu
from jax.sharding import PartitionSpec as P

HD = 128
BLK = 512
TOPK = 3
HALF = 64
PART = 4
ROWS = PART * HALF
KEYS = 2 * (TOPK + 1) * ROWS
WIDE = 32
GROUP = 7
MIB = 1024 * 1024

BF = jnp.bfloat16
F32 = jnp.float32
NN = ((1,), (0,))
SMEM = pl.BlockSpec(memory_space=pltpu.SMEM)
ANY = pl.BlockSpec(memory_space=pl.ANY)


def dot(a, b):
    return lax.dot_general(a, b, (NN, ((), ())), preferred_element_type=F32)


def call(kernel, name, out_shape, n_smem, n_any, scratch, vmem, moved, flops=0, aliases=None):
    one = not isinstance(out_shape, list)
    return pl.pallas_call(
        kernel,
        in_specs=[SMEM] * n_smem + [ANY] * n_any,
        out_specs=ANY if one else [ANY] * len(out_shape),
        out_shape=out_shape,
        scratch_shapes=scratch,
        input_output_aliases=aliases or {},
        compiler_params=pltpu.CompilerParams(vmem_limit_bytes=vmem * MIB),
        cost_estimate=pl.CostEstimate(flops=flops, bytes_accessed=moved, transcendentals=0),
        name=name,
    )


def spread(core, arrays, base, whole=None):
    heads = arrays[0].shape[-1] // HD
    groups = heads // GROUP

    def kernel(place_ref, *refs):
        sources = refs[:4] if len(arrays) == 4 else [refs[0].at[a] for a in range(4)]
        out_ref, got, cut, in_sem, out_sem = refs[-5:]

        def load(g, a):
            return pltpu.make_async_copy(
                sources[a].at[0:HALF, pl.ds(g * GROUP * HD, GROUP * HD)], got.at[g, a], in_sem.at[g, a]
            )

        def store(g):
            at = pl.ds(place_ref[0] * WIDE + g * GROUP, GROUP)
            return pltpu.make_async_copy(cut.at[pl.ds(g * GROUP, GROUP)], out_ref.at[at], out_sem.at[g])

        for g in range(groups):
            for a in range(4):
                load(g, a).start()
        for g in range(groups):
            for a in range(4):
                load(g, a).wait()
                for h in range(GROUP):
                    cut[g * GROUP + h, a] = got[g, a, :, h * HD : (h + 1) * HD]
            store(g).start()
        for g in range(groups):
            store(g).wait()

    extra = [] if whole is None else [whole]
    return call(
        kernel, "spread_heads",
        jax.ShapeDtypeStruct((2 * WIDE, 4, HALF, HD), BF), 1, len(arrays) + len(extra),
        [
            pltpu.VMEM((groups, 4, HALF, GROUP * HD), BF),
            pltpu.VMEM((heads, 4, HALF, HD), BF),
            pltpu.SemaphoreType.DMA((groups, 4)),
            pltpu.SemaphoreType.DMA((groups,)),
        ],
        50 if extra else 56, 4 << 20, aliases={1 + len(arrays): 0} if extra else None,
    )(base[None], *arrays, *extra)


def attend_kernel(
    place_ref, picks_ref, own_hbm, other_hbm,
    first_hbm, mine_hbm, theirs_hbm,
    own_ref, other_ref, kt_ref, vt_ref, s0_ref, s1_ref, t0_ref, t1_ref, low_ref, ds_ref,
    mine_ref, sum_ref, theirs_ref, first_ref, in_sem, first_sem, mine_sem, theirs_sem,
):
    nb = picks_ref.shape[0]
    half_at, seg = place_ref[0], place_ref[1]
    scale = 1.0 / math.sqrt(HD)
    power = scale * math.log2(math.e)
    s_refs, t_refs = (s0_ref, s1_ref), (t0_ref, t1_ref)
    chunks = [(j, half) for j in range(TOPK + 1) for half in range(2)]
    rows = [pl.ds(n * ROWS, ROWS) for n in range(len(chunks))]

    def loads(b):
        at = pl.ds(b * PART, PART)
        return (
            pltpu.make_async_copy(own_hbm.at[at], own_ref.at[at], in_sem.at[b, 0]),
            pltpu.make_async_copy(other_hbm.at[at], other_ref.at[at], in_sem.at[b, 1]),
        )

    def start(b, carry):
        for copy in loads(b):
            copy.start()
        return carry

    def arrive(b):
        for copy in loads(b):
            copy.wait()

    def part(a, half, b):
        ref = own_ref if half == 0 else other_ref
        return ref[pl.ds(b * PART, PART), a].reshape(ROWS, HD)

    def slots_of(i):
        return [picks_ref[i, j] for j in range(TOPK)] + [i]

    def turn(b):
        for half in range(2):
            kt_ref[half * nb + b] = part(0, half, b).T
            vt_ref[half * nb + b] = part(1, half, b).T

    def scores(i, buf):
        qt = part(2, 0, i).T
        slots = slots_of(i)
        key_at = lax.broadcasted_iota(jnp.int32, (ROWS, ROWS), 0)
        query_at = lax.broadcasted_iota(jnp.int32, (ROWS, ROWS), 1)
        top = jnp.full((1, ROWS), -jnp.inf, F32)
        for n, (j, half) in enumerate(chunks):
            s = dot(part(0, half, slots[j]), qt)
            if j < TOPK:
                valid = slots[j] < i
            elif half == 0:
                valid = key_at <= query_at
            else:
                valid = key_at // HALF < query_at // HALF + half_at
            s = jnp.where(valid, s, -jnp.inf)
            s_refs[buf][rows[n]] = s
            top = jnp.maximum(top, jnp.max(s, axis=0, keepdims=True))
        t_refs[buf][...] = jnp.broadcast_to(top, (8, ROWS))

    def add_terms(a, terms, slots):
        for n, (j, half) in enumerate(chunks):
            acc = mine_ref if half == 0 else sum_ref
            at = pl.ds(slots[j] * PART, PART)
            term = terms[n * ROWS : (n + 1) * ROWS].reshape(PART, HALF, HD)
            if j < TOPK:
                acc[a, at] += term
            else:
                acc[a, at] = term

    def flat(ref, slots):
        return jnp.concatenate([ref[half * nb + slots[j]] for j, half in chunks], axis=1)

    def rest(i, buf):
        s_ref = s_refs[buf]
        q, g = part(2, 0, i), part(3, 0, i)
        gt = g.T
        slots = slots_of(i)
        top = t_refs[buf][0:1]
        total = jnp.zeros((1, ROWS), F32)
        for n in range(len(chunks)):
            e = jnp.exp2((s_ref[rows[n]] - top) * power)
            s_ref[rows[n]] = e
            total = total + jnp.sum(e, axis=0, keepdims=True)
        inverse = 1.0 / total
        for n in range(len(chunks)):
            low_ref[rows[n]] = (s_ref[rows[n]] * inverse).astype(BF)
        out_t = dot(flat(vt_ref, slots), low_ref[...])
        add_terms(1, dot(low_ref[...], g), slots)
        out = out_t.T.astype(BF)
        delta = jnp.sum(gt.astype(F32) * out_t.astype(BF).astype(F32), axis=0, keepdims=True)
        for n, (j, half) in enumerate(chunks):
            dp = dot(part(1, half, slots[j]), gt)
            ds_ref[rows[n]] = (s_ref[rows[n]] * inverse * (dp - delta)).astype(BF)
        query_t = dot(flat(kt_ref, slots), ds_ref[...])
        add_terms(0, dot(ds_ref[...], q), slots)
        query = (query_t * scale).T.astype(BF)
        first = jnp.where(seg == 0, out.astype(F32), query.astype(F32)).astype(BF)
        first_ref[pl.ds(i * PART, PART)] = first.reshape(PART, HALF, HD)

    def send_first(p):
        at = pl.ds(p * 2 * PART, 2 * PART)
        return pltpu.make_async_copy(first_ref.at[at], first_hbm.at[at, 0], first_sem.at[p])

    lax.fori_loop(0, nb, start, 0)
    arrive(0)
    turn(0)
    scores(0, 0)

    def pair(p, carry):
        i = 2 * p
        later = jnp.minimum(i + 2, nb - 1)
        arrive(i + 1)

        @pl.when(i + 2 < nb)
        def _():
            arrive(i + 2)

        turn(i + 1)
        turn(later)
        scores(i + 1, 1)
        rest(i, 0)
        scores(later, 0)
        rest(i + 1, 1)
        send_first(p).start()
        return carry

    lax.fori_loop(0, nb // 2, pair, 0)

    def send_mine(a):
        return pltpu.make_async_copy(mine_ref.at[a], mine_hbm.at[a], mine_sem.at[a])

    def send_theirs(b):
        at = pl.ds(b * 4 * PART, 4 * PART)
        return pltpu.make_async_copy(theirs_ref.at[:, at], theirs_hbm.at[:, at], theirs_sem.at[b])

    for a in range(2):
        send_mine(a).start()
    for b in range(nb // 4):
        at = pl.ds(b * 4 * PART, 4 * PART)
        for a in range(2):
            theirs_ref[a, at] = sum_ref[a, at].astype(BF)
        send_theirs(b).start()
    for p in range(nb // 2):
        send_first(p).wait()
    for a in range(2):
        send_mine(a).wait()
    for b in range(nb // 4):
        send_theirs(b).wait()


def attend(place, picks, own, other):
    nb = picks.shape[0]
    n = nb * PART
    work = 6 * 2 * nb * ROWS * KEYS * HD
    return call(
        attend_kernel, "attend_head",
        [
            jax.ShapeDtypeStruct((n, 3, HALF, HD), BF),
            jax.ShapeDtypeStruct((2, n, HALF, HD), F32),
            jax.ShapeDtypeStruct((2, n, HALF, HD), BF),
        ],
        2, 2,
        [
            pltpu.VMEM((n, 4, HALF, HD), BF),
            pltpu.VMEM((n, 2, HALF, HD), BF),
            pltpu.VMEM((2 * nb, HD, ROWS), BF),
            pltpu.VMEM((2 * nb, HD, ROWS), BF),
            pltpu.VMEM((KEYS, ROWS), F32),
            pltpu.VMEM((KEYS, ROWS), F32),
            pltpu.VMEM((8, ROWS), F32),
            pltpu.VMEM((8, ROWS), F32),
            pltpu.VMEM((KEYS, ROWS), BF),
            pltpu.VMEM((KEYS, ROWS), BF),
            pltpu.VMEM((2, n, HALF, HD), F32),
            pltpu.VMEM((2, n, HALF, HD), F32),
            pltpu.VMEM((2, n, HALF, HD), BF),
            pltpu.VMEM((n, HALF, HD), BF),
            pltpu.SemaphoreType.DMA((nb, 2)),
            pltpu.SemaphoreType.DMA((nb // 2,)),
            pltpu.SemaphoreType.DMA((2,)),
            pltpu.SemaphoreType.DMA((nb // 4,)),
        ],
        42, 16 << 20, work,
    )(place, picks, own, other)


def combine(whole, mine, got):
    n = whole.shape[0]
    groups = 4
    size = n // groups

    def kernel(whole_ref, mine_hbm, got_hbm, out_hbm, mine_ref, got_ref, out_ref, in_sem, out_sem):
        scale = 1.0 / math.sqrt(HD)
        at = [pl.ds(g * size, size) for g in range(groups)]

        def loads(g):
            return (
                pltpu.make_async_copy(mine_hbm.at[:, at[g]], mine_ref.at[:, at[g]], in_sem.at[g, 0]),
                pltpu.make_async_copy(got_hbm.at[:, at[g]], got_ref.at[:, at[g]], in_sem.at[g, 1]),
            )

        def store(g):
            return pltpu.make_async_copy(out_ref.at[at[g]], out_hbm.at[at[g], 1:3], out_sem.at[g])

        for g in range(groups):
            for copy in loads(g):
                copy.start()
        for g in range(groups):
            for copy in loads(g):
                copy.wait()
            for a in range(2):
                value = mine_ref[a, at[g]] + got_ref[a, at[g]].astype(F32)
                out_ref[at[g], a] = (value * scale if a == 0 else value).astype(BF)
            store(g).start()
        for g in range(groups):
            store(g).wait()

    return call(
        kernel, "combine_halves", jax.ShapeDtypeStruct(whole.shape, BF), 0, 3,
        [
            pltpu.VMEM((2, n, HALF, HD), F32),
            pltpu.VMEM((2, n, HALF, HD), BF),
            pltpu.VMEM((n, 2, HALF, HD), BF),
            pltpu.SemaphoreType.DMA((groups, 2)),
            pltpu.SemaphoreType.DMA((groups,)),
        ],
        12, 8 << 20, aliases={0: 0},
    )(whole, mine, got)


def gather(core, source, base, high, results=None):
    heads = 4 * GROUP
    groups = heads // GROUP
    rows = slice(HALF, 2 * HALF) if high else slice(0, HALF)

    def kernel(place_ref, source_ref, *refs):
        outs = refs[-8:-4]
        got, cut, in_sem, out_sem = refs[-4:]

        def load(g):
            at = pl.ds(place_ref[1] + g * GROUP, GROUP)
            return pltpu.make_async_copy(source_ref.at[at], got.at[g], in_sem.at[g])

        def store(g, a):
            cols = pl.ds(g * GROUP * HD, GROUP * HD)
            return pltpu.make_async_copy(cut.at[g, a], outs[a].at[0, rows, cols], out_sem.at[g, a])

        for g in range(groups):
            load(g).start()
        for g in range(groups):
            load(g).wait()
            for a in range(4):
                live = place_ref[0] == (1 if a == 0 else 0)
                for h in range(GROUP):
                    value = got[g, h, max(a - 1, 0)]
                    cut[g, a, :, h * HD : (h + 1) * HD] = jnp.where(live, value, jnp.zeros_like(value))
                store(g, a).start()
        for g in range(groups):
            for a in range(4):
                store(g, a).wait()

    extra = [] if results is None else list(results)
    return call(
        kernel, "gather_heads", [jax.ShapeDtypeStruct((1, 2 * HALF, heads * HD), BF)] * 4, 1, 1 + len(extra),
        [
            pltpu.VMEM((groups, GROUP, 3, HALF, HD), BF),
            pltpu.VMEM((groups, 4, HALF, GROUP * HD), BF),
            pltpu.SemaphoreType.DMA((groups,)),
            pltpu.SemaphoreType.DMA((groups, 4)),
        ],
        8, 4 << 20, aliases={2 + a: a for a in range(4)} if extra else None,
    )(jnp.stack([core, base]), source, *extra)


def cut_out(name, out_shape, vmem, pieces, place, *sources):
    def kernel(place_ref, *refs):
        out_ref, held, in_sem, out_sem = refs[-4:]
        copies = []
        for n, (src, at) in enumerate(pieces(place_ref, refs[:-4])):
            there = pltpu.make_async_copy(src, held.at[at], in_sem.at[n])
            copies.append((there, pltpu.make_async_copy(held.at[at], out_ref.at[at], out_sem.at[n])))
        for there, _ in copies:
            there.start()
        for there, back in copies:
            there.wait()
            back.start()
        for _, back in copies:
            back.wait()

    return call(
        kernel, name, jax.ShapeDtypeStruct(out_shape, BF), 1, len(sources),
        [pltpu.VMEM(out_shape, BF), pltpu.SemaphoreType.DMA((4,)), pltpu.SemaphoreType.DMA((4,))],
        vmem, 2 << 20,
    )(place[None], *sources)


CHIPS = ("ctx", "tp")
SWAP = [(0, 1), (1, 0)]


def on_device(queries, keys, values, out_grad, chosen):
    heads = queries.shape[2] // HD
    core = lax.axis_index("pipe").astype(jnp.int32)
    seg = (lax.axis_index(CHIPS) // WIDE).astype(jnp.int32)

    place = jnp.stack([core ^ seg, seg])
    arrays = (keys, values, queries, out_grad)
    theirs = cut_out(
        "cut_tokens", (4, HALF, heads * HD), 56,
        lambda _, refs: [(ref.at[0, HALF : 2 * HALF], a) for a, ref in enumerate(refs)],
        core, *arrays,
    )
    got = lax.ppermute(theirs, "pipe", SWAP)
    other_chosen = lax.ppermute(chosen, "pipe", SWAP)
    parts = spread(core, [x[0] for x in arrays], core)
    parts = spread(core, [got], 1 - core, parts)
    picks = jnp.where(seg == core, chosen, other_chosen)[0]
    parts, picks, place = lax.optimization_barrier((parts, picks, place))

    own = lax.all_to_all(parts, CHIPS, 0, 0, tiled=True)
    n = own.shape[0]
    mine = cut_out(
        "cut_keys", (n, 2, HALF, HD), 56,
        lambda _, refs: [
            (refs[0].at[pl.ds(g * n // 4, n // 4), 0:2], pl.ds(g * n // 4, n // 4)) for g in range(4)
        ],
        core, own,
    )
    other = lax.ppermute(mine, "pipe", SWAP)
    first, mine, theirs = attend(place, picks, own, other)
    whole = combine(first, mine, lax.ppermute(theirs, "pipe", SWAP))

    back = lax.all_to_all(whole, CHIPS, 0, 0, tiled=True)
    theirs = cut_out(
        "cut_heads", (heads, 3, HALF, HD), 4,
        lambda place_ref, refs: [
            (refs[0].at[pl.ds(place_ref[0] * WIDE + g * GROUP, GROUP)], pl.ds(g * GROUP, GROUP)) for g in range(4)
        ],
        core, back,
    )
    got = lax.ppermute(theirs, "pipe", SWAP)
    results = gather(core, back, (1 - core) * WIDE, True)
    return tuple(gather(core, got, core * 0, False, results))


def solution(mesh):
    placed = P("pipe", CHIPS, None)
    return jax.shard_map(
        on_device,
        mesh=mesh,
        in_specs=(placed,) * 4 + (P("pipe", None, None),),
        out_specs=(placed,) * 4,
        check_vma=False,
    )
```

```python
import math

import jax
import jax.numpy as jnp
from jax import lax
from jax.experimental import pallas as pl
from jax.experimental.pallas import tpu as pltpu
from jax.sharding import PartitionSpec as P

HD = 128
BLK = 512
TOPK = 3
HALF = 64
PART = 4
ROWS = PART * HALF
KEYS = 2 * (TOPK + 1) * ROWS
WIDE = 32
GROUP = 7
MIB = 1024 * 1024

BF = jnp.bfloat16
F32 = jnp.float32
NN = ((1,), (0,))
SMEM = pl.BlockSpec(memory_space=pltpu.SMEM)
ANY = pl.BlockSpec(memory_space=pl.ANY)


def dot(a, b):
    return lax.dot_general(a, b, (NN, ((), ())), preferred_element_type=F32)


def call(kernel, name, out_shape, n_smem, n_any, scratch, vmem, moved, flops=0, aliases=None):
    one = not isinstance(out_shape, list)
    return pl.pallas_call(
        kernel,
        in_specs=[SMEM] * n_smem + [ANY] * n_any,
        out_specs=ANY if one else [ANY] * len(out_shape),
        out_shape=out_shape,
        scratch_shapes=scratch,
        input_output_aliases=aliases or {},
        compiler_params=pltpu.CompilerParams(vmem_limit_bytes=vmem * MIB),
        cost_estimate=pl.CostEstimate(flops=flops, bytes_accessed=moved, transcendentals=0),
        name=name,
    )


def spread(core, arrays, base, whole=None):
    heads = arrays[0].shape[-1] // HD
    groups = heads // GROUP

    def kernel(place_ref, *refs):
        sources = refs[:4] if len(arrays) == 4 else [refs[0].at[a] for a in range(4)]
        out_ref, got, cut, in_sem, out_sem = refs[-5:]

        def load(g, a):
            return pltpu.make_async_copy(
                sources[a].at[0:HALF, pl.ds(g * GROUP * HD, GROUP * HD)], got.at[g, a], in_sem.at[g, a]
            )

        def store(g):
            at = pl.ds(place_ref[0] * WIDE + g * GROUP, GROUP)
            return pltpu.make_async_copy(cut.at[pl.ds(g * GROUP, GROUP)], out_ref.at[at], out_sem.at[g])

        for g in range(groups):
            for a in range(4):
                load(g, a).start()
        for g in range(groups):
            for a in range(4):
                load(g, a).wait()
                for h in range(GROUP):
                    cut[g * GROUP + h, a] = got[g, a, :, h * HD : (h + 1) * HD]
            store(g).start()
        for g in range(groups):
            store(g).wait()

    extra = [] if whole is None else [whole]
    return call(
        kernel, "spread_heads",
        jax.ShapeDtypeStruct((2 * WIDE, 4, HALF, HD), BF), 1, len(arrays) + len(extra),
        [
            pltpu.VMEM((groups, 4, HALF, GROUP * HD), BF),
            pltpu.VMEM((heads, 4, HALF, HD), BF),
            pltpu.SemaphoreType.DMA((groups, 4)),
            pltpu.SemaphoreType.DMA((groups,)),
        ],
        50 if extra else 56, 4 << 20, aliases={1 + len(arrays): 0} if extra else None,
    )(base[None], *arrays, *extra)


def attend_kernel(
    place_ref, picks_ref, own_hbm, other_hbm,
    first_hbm, mine_hbm, theirs_hbm,
    own_ref, other_ref, kt_ref, vt_ref, s0_ref, s1_ref, t0_ref, t1_ref, d_ref, low_ref, ds_ref,
    mine_ref, sum_ref, theirs_ref, first_ref, in_sem, first_sem, mine_sem, theirs_sem,
):
    nb = picks_ref.shape[0]
    half_at, seg = place_ref[0], place_ref[1]
    scale = 1.0 / math.sqrt(HD)
    power = scale * math.log2(math.e)
    s_refs, t_refs = (s0_ref, s1_ref), (t0_ref, t1_ref)
    chunks = [(j, half) for j in range(TOPK + 1) for half in range(2)]
    rows = [pl.ds(n * ROWS, ROWS) for n in range(len(chunks))]

    def loads(b):
        at = pl.ds(b * PART, PART)
        return (
            pltpu.make_async_copy(own_hbm.at[at], own_ref.at[at], in_sem.at[b, 0]),
            pltpu.make_async_copy(other_hbm.at[at], other_ref.at[at], in_sem.at[b, 1]),
        )

    def start(b, carry):
        for copy in loads(b):
            copy.start()
        return carry

    def arrive(b):
        for copy in loads(b):
            copy.wait()

    def part(a, half, b):
        ref = own_ref if half == 0 else other_ref
        return ref[pl.ds(b * PART, PART), a].reshape(ROWS, HD)

    def slots_of(i):
        return [picks_ref[i, j] for j in range(TOPK)] + [i]

    def turn(b):
        for half in range(2):
            kt_ref[half * nb + b] = part(0, half, b).T
            vt_ref[half * nb + b] = part(1, half, b).T

    def scores(i, buf):
        qt = part(2, 0, i).T
        slots = slots_of(i)
        key_at = lax.broadcasted_iota(jnp.int32, (ROWS, ROWS), 0)
        query_at = lax.broadcasted_iota(jnp.int32, (ROWS, ROWS), 1)
        top = jnp.full((8, ROWS), -jnp.inf, F32)
        for n, (j, half) in enumerate(chunks):
            s = dot(part(0, half, slots[j]), qt)
            if j < TOPK:
                valid = slots[j] < i
            elif half == 0:
                valid = key_at <= query_at
            else:
                valid = key_at // HALF < query_at // HALF + half_at
            s = jnp.where(valid, s, -jnp.inf)
            s_refs[buf][rows[n]] = s
            top = jnp.maximum(top, jnp.max(s.reshape(ROWS // 8, 8, ROWS), axis=0))
        t_refs[buf][...] = jnp.broadcast_to(jnp.max(top, axis=0, keepdims=True), (8, ROWS))

    def add_terms(a, terms, slots):
        for n, (j, half) in enumerate(chunks):
            acc = mine_ref if half == 0 else sum_ref
            at = pl.ds(slots[j] * PART, PART)
            term = terms[n * ROWS : (n + 1) * ROWS].reshape(PART, HALF, HD)
            if j < TOPK:
                acc[a, at] += term
            else:
                acc[a, at] = term

    def flat(ref, slots):
        return jnp.concatenate([ref[half * nb + slots[j]] for j, half in chunks], axis=1)

    def rest(i, buf):
        s_ref = s_refs[buf]
        q, g = part(2, 0, i), part(3, 0, i)
        gt = g.T
        slots = slots_of(i)
        top = t_refs[buf][...]
        total = jnp.zeros((8, ROWS), F32)
        for n in range(len(chunks)):
            e = jnp.exp2((s_ref[rows[n]].reshape(ROWS // 8, 8, ROWS) - top) * power)
            s_ref[rows[n]] = e.reshape(ROWS, ROWS)
            total = total + jnp.sum(e, axis=0)
        t_refs[buf][...] = jnp.broadcast_to(1.0 / jnp.sum(total, axis=0, keepdims=True), (8, ROWS))
        inverse = t_refs[buf][...]
        for n in range(len(chunks)):
            low = s_ref[rows[n]].reshape(ROWS // 8, 8, ROWS) * inverse
            low_ref[rows[n]] = low.reshape(ROWS, ROWS).astype(BF)
        out_t = dot(flat(vt_ref, slots), low_ref[...])
        add_terms(1, dot(low_ref[...], g), slots)
        out = out_t.T.astype(BF)
        delta = jnp.sum(gt.astype(F32) * out_t.astype(BF).astype(F32), axis=0, keepdims=True)
        d_ref[...] = jnp.broadcast_to(delta, (8, ROWS))
        delta = d_ref[...]
        for n, (j, half) in enumerate(chunks):
            dp = dot(part(1, half, slots[j]), gt).reshape(ROWS // 8, 8, ROWS)
            ds = s_ref[rows[n]].reshape(ROWS // 8, 8, ROWS) * inverse * (dp - delta)
            ds_ref[rows[n]] = ds.reshape(ROWS, ROWS).astype(BF)
        query_t = dot(flat(kt_ref, slots), ds_ref[...])
        add_terms(0, dot(ds_ref[...], q), slots)
        query = (query_t * scale).T.astype(BF)
        first = jnp.where(seg == 0, out.astype(F32), query.astype(F32)).astype(BF)
        first_ref[pl.ds(i * PART, PART)] = first.reshape(PART, HALF, HD)

    def send_first(p):
        at = pl.ds(p * 2 * PART, 2 * PART)
        return pltpu.make_async_copy(first_ref.at[at], first_hbm.at[at, 0], first_sem.at[p])

    lax.fori_loop(0, nb, start, 0)
    arrive(0)
    turn(0)
    scores(0, 0)

    def pair(p, carry):
        i = 2 * p
        later = jnp.minimum(i + 2, nb - 1)
        arrive(i + 1)

        @pl.when(i + 2 < nb)
        def _():
            arrive(i + 2)

        turn(i + 1)
        turn(later)
        scores(i + 1, 1)
        rest(i, 0)
        scores(later, 0)
        rest(i + 1, 1)
        send_first(p).start()
        return carry

    lax.fori_loop(0, nb // 2, pair, 0)

    def send_mine(a):
        return pltpu.make_async_copy(mine_ref.at[a], mine_hbm.at[a], mine_sem.at[a])

    def send_theirs(b):
        at = pl.ds(b * 4 * PART, 4 * PART)
        return pltpu.make_async_copy(theirs_ref.at[:, at], theirs_hbm.at[:, at], theirs_sem.at[b])

    for a in range(2):
        send_mine(a).start()
    for b in range(nb // 4):
        at = pl.ds(b * 4 * PART, 4 * PART)
        for a in range(2):
            theirs_ref[a, at] = sum_ref[a, at].astype(BF)
        send_theirs(b).start()
    for p in range(nb // 2):
        send_first(p).wait()
    for a in range(2):
        send_mine(a).wait()
    for b in range(nb // 4):
        send_theirs(b).wait()


def attend(place, picks, own, other):
    nb = picks.shape[0]
    n = nb * PART
    work = 6 * 2 * nb * ROWS * KEYS * HD
    return call(
        attend_kernel, "attend_head",
        [
            jax.ShapeDtypeStruct((n, 3, HALF, HD), BF),
            jax.ShapeDtypeStruct((2, n, HALF, HD), F32),
            jax.ShapeDtypeStruct((2, n, HALF, HD), BF),
        ],
        2, 2,
        [
            pltpu.VMEM((n, 4, HALF, HD), BF),
            pltpu.VMEM((n, 2, HALF, HD), BF),
            pltpu.VMEM((2 * nb, HD, ROWS), BF),
            pltpu.VMEM((2 * nb, HD, ROWS), BF),
            pltpu.VMEM((KEYS, ROWS), F32),
            pltpu.VMEM((KEYS, ROWS), F32),
            pltpu.VMEM((8, ROWS), F32),
            pltpu.VMEM((8, ROWS), F32),
            pltpu.VMEM((8, ROWS), F32),
            pltpu.VMEM((KEYS, ROWS), BF),
            pltpu.VMEM((KEYS, ROWS), BF),
            pltpu.VMEM((2, n, HALF, HD), F32),
            pltpu.VMEM((2, n, HALF, HD), F32),
            pltpu.VMEM((2, n, HALF, HD), BF),
            pltpu.VMEM((n, HALF, HD), BF),
            pltpu.SemaphoreType.DMA((nb, 2)),
            pltpu.SemaphoreType.DMA((nb // 2,)),
            pltpu.SemaphoreType.DMA((2,)),
            pltpu.SemaphoreType.DMA((nb // 4,)),
        ],
        42, 16 << 20, work,
    )(place, picks, own, other)


def combine(whole, mine, got):
    n = whole.shape[0]
    groups = 4
    size = n // groups

    def kernel(whole_ref, mine_hbm, got_hbm, out_hbm, mine_ref, got_ref, out_ref, in_sem, out_sem):
        scale = 1.0 / math.sqrt(HD)
        at = [pl.ds(g * size, size) for g in range(groups)]

        def loads(g):
            return (
                pltpu.make_async_copy(mine_hbm.at[:, at[g]], mine_ref.at[:, at[g]], in_sem.at[g, 0]),
                pltpu.make_async_copy(got_hbm.at[:, at[g]], got_ref.at[:, at[g]], in_sem.at[g, 1]),
            )

        def store(g):
            return pltpu.make_async_copy(out_ref.at[at[g]], out_hbm.at[at[g], 1:3], out_sem.at[g])

        for g in range(groups):
            for copy in loads(g):
                copy.start()
        for g in range(groups):
            for copy in loads(g):
                copy.wait()
            for a in range(2):
                value = mine_ref[a, at[g]] + got_ref[a, at[g]].astype(F32)
                out_ref[at[g], a] = (value * scale if a == 0 else value).astype(BF)
            store(g).start()
        for g in range(groups):
            store(g).wait()

    return call(
        kernel, "combine_halves", jax.ShapeDtypeStruct(whole.shape, BF), 0, 3,
        [
            pltpu.VMEM((2, n, HALF, HD), F32),
            pltpu.VMEM((2, n, HALF, HD), BF),
            pltpu.VMEM((n, 2, HALF, HD), BF),
            pltpu.SemaphoreType.DMA((groups, 2)),
            pltpu.SemaphoreType.DMA((groups,)),
        ],
        12, 8 << 20, aliases={0: 0},
    )(whole, mine, got)


def gather(core, source, base, high, results=None):
    heads = 4 * GROUP
    groups = heads // GROUP
    rows = slice(HALF, 2 * HALF) if high else slice(0, HALF)

    def kernel(place_ref, source_ref, *refs):
        outs = refs[-8:-4]
        got, cut, in_sem, out_sem = refs[-4:]

        def load(g):
            at = pl.ds(place_ref[1] + g * GROUP, GROUP)
            return pltpu.make_async_copy(source_ref.at[at], got.at[g], in_sem.at[g])

        def store(g, a):
            cols = pl.ds(g * GROUP * HD, GROUP * HD)
            return pltpu.make_async_copy(cut.at[g, a], outs[a].at[0, rows, cols], out_sem.at[g, a])

        for g in range(groups):
            load(g).start()
        for g in range(groups):
            load(g).wait()
            for a in range(4):
                live = place_ref[0] == (1 if a == 0 else 0)
                for h in range(GROUP):
                    value = got[g, h, max(a - 1, 0)]
                    cut[g, a, :, h * HD : (h + 1) * HD] = jnp.where(live, value, jnp.zeros_like(value))
                store(g, a).start()
        for g in range(groups):
            for a in range(4):
                store(g, a).wait()

    extra = [] if results is None else list(results)
    return call(
        kernel, "gather_heads", [jax.ShapeDtypeStruct((1, 2 * HALF, heads * HD), BF)] * 4, 1, 1 + len(extra),
        [
            pltpu.VMEM((groups, GROUP, 3, HALF, HD), BF),
            pltpu.VMEM((groups, 4, HALF, GROUP * HD), BF),
            pltpu.SemaphoreType.DMA((groups,)),
            pltpu.SemaphoreType.DMA((groups, 4)),
        ],
        8, 4 << 20, aliases={2 + a: a for a in range(4)} if extra else None,
    )(jnp.stack([core, base]), source, *extra)


def cut_out(name, out_shape, vmem, pieces, place, *sources):
    def kernel(place_ref, *refs):
        out_ref, held, in_sem, out_sem = refs[-4:]
        copies = []
        for n, (src, at) in enumerate(pieces(place_ref, refs[:-4])):
            there = pltpu.make_async_copy(src, held.at[at], in_sem.at[n])
            copies.append((there, pltpu.make_async_copy(held.at[at], out_ref.at[at], out_sem.at[n])))
        for there, _ in copies:
            there.start()
        for there, back in copies:
            there.wait()
            back.start()
        for _, back in copies:
            back.wait()

    return call(
        kernel, name, jax.ShapeDtypeStruct(out_shape, BF), 1, len(sources),
        [pltpu.VMEM(out_shape, BF), pltpu.SemaphoreType.DMA((4,)), pltpu.SemaphoreType.DMA((4,))],
        vmem, 2 << 20,
    )(place[None], *sources)


CHIPS = ("ctx", "tp")
SWAP = [(0, 1), (1, 0)]


def on_device(queries, keys, values, out_grad, chosen):
    heads = queries.shape[2] // HD
    core = lax.axis_index("pipe").astype(jnp.int32)
    seg = (lax.axis_index(CHIPS) // WIDE).astype(jnp.int32)

    place = jnp.stack([core ^ seg, seg])
    arrays = (keys, values, queries, out_grad)
    theirs = cut_out(
        "cut_tokens", (4, HALF, heads * HD), 56,
        lambda _, refs: [(ref.at[0, HALF : 2 * HALF], a) for a, ref in enumerate(refs)],
        core, *arrays,
    )
    got = lax.ppermute(theirs, "pipe", SWAP)
    other_chosen = lax.ppermute(chosen, "pipe", SWAP)
    parts = spread(core, [x[0] for x in arrays], core)
    parts = spread(core, [got], 1 - core, parts)
    picks = jnp.where(seg == core, chosen, other_chosen)[0]
    parts, picks, place = lax.optimization_barrier((parts, picks, place))

    own = lax.all_to_all(parts, CHIPS, 0, 0, tiled=True)
    n = own.shape[0]
    mine = cut_out(
        "cut_keys", (n, 2, HALF, HD), 50,
        lambda _, refs: [
            (refs[0].at[pl.ds(g * n // 4, n // 4), 0:2], pl.ds(g * n // 4, n // 4)) for g in range(4)
        ],
        core, own,
    )
    other = lax.ppermute(mine, "pipe", SWAP)
    first, mine, theirs = attend(place, picks, own, other)
    whole = combine(first, mine, lax.ppermute(theirs, "pipe", SWAP))

    back = lax.all_to_all(whole, CHIPS, 0, 0, tiled=True)
    theirs = cut_out(
        "cut_heads", (heads, 3, HALF, HD), 4,
        lambda place_ref, refs: [
            (refs[0].at[pl.ds(place_ref[0] * WIDE + g * GROUP, GROUP)], pl.ds(g * GROUP, GROUP)) for g in range(4)
        ],
        core, back,
    )
    got = lax.ppermute(theirs, "pipe", SWAP)
    results = gather(core, back, (1 - core) * WIDE, True)
    return tuple(gather(core, got, core * 0, False, results))


def solution(mesh):
    placed = P("pipe", CHIPS, None)
    return jax.shard_map(
        on_device,
        mesh=mesh,
        in_specs=(placed,) * 4 + (P("pipe", None, None),),
        out_specs=(placed,) * 4,
        check_vma=False,
    )
```

```python
import math

import jax
import jax.numpy as jnp
from jax import lax
from jax.experimental import pallas as pl
from jax.experimental.pallas import tpu as pltpu
from jax.sharding import PartitionSpec as P

HD = 128
BLK = 512
TOPK = 3
HALF = 64
PART = 4
ROWS = PART * HALF
KEYS = 2 * (TOPK + 1) * ROWS
WIDE = 32
GROUP = 7
MIB = 1024 * 1024

BF = jnp.bfloat16
F32 = jnp.float32
NN = ((1,), (0,))
SMEM = pl.BlockSpec(memory_space=pltpu.SMEM)
ANY = pl.BlockSpec(memory_space=pl.ANY)


def dot(a, b):
    return lax.dot_general(a, b, (NN, ((), ())), preferred_element_type=F32)


def call(kernel, name, out_shape, n_smem, n_any, scratch, vmem, moved, flops=0, aliases=None):
    one = not isinstance(out_shape, list)
    return pl.pallas_call(
        kernel,
        in_specs=[SMEM] * n_smem + [ANY] * n_any,
        out_specs=ANY if one else [ANY] * len(out_shape),
        out_shape=out_shape,
        scratch_shapes=scratch,
        input_output_aliases=aliases or {},
        compiler_params=pltpu.CompilerParams(vmem_limit_bytes=vmem * MIB),
        cost_estimate=pl.CostEstimate(flops=flops, bytes_accessed=moved, transcendentals=0),
        name=name,
    )


def spread(core, arrays, base, whole=None):
    heads = arrays[0].shape[-1] // HD
    groups = heads // GROUP

    def kernel(place_ref, *refs):
        sources = refs[:4] if len(arrays) == 4 else [refs[0].at[a] for a in range(4)]
        out_ref, got, cut, in_sem, out_sem = refs[-5:]

        def load(g, a):
            return pltpu.make_async_copy(
                sources[a].at[0:HALF, pl.ds(g * GROUP * HD, GROUP * HD)], got.at[g, a], in_sem.at[g, a]
            )

        def store(g):
            at = pl.ds(place_ref[0] * WIDE + g * GROUP, GROUP)
            return pltpu.make_async_copy(cut.at[pl.ds(g * GROUP, GROUP)], out_ref.at[at], out_sem.at[g])

        for g in range(groups):
            for a in range(4):
                load(g, a).start()
        for g in range(groups):
            for a in range(4):
                load(g, a).wait()
                for h in range(GROUP):
                    cut[g * GROUP + h, a] = got[g, a, :, h * HD : (h + 1) * HD]
            store(g).start()
        for g in range(groups):
            store(g).wait()

    extra = [] if whole is None else [whole]
    return call(
        kernel, "spread_heads",
        jax.ShapeDtypeStruct((2 * WIDE, 4, HALF, HD), BF), 1, len(arrays) + len(extra),
        [
            pltpu.VMEM((groups, 4, HALF, GROUP * HD), BF),
            pltpu.VMEM((heads, 4, HALF, HD), BF),
            pltpu.SemaphoreType.DMA((groups, 4)),
            pltpu.SemaphoreType.DMA((groups,)),
        ],
        50 if extra else 56, 4 << 20, aliases={1 + len(arrays): 0} if extra else None,
    )(base[None], *arrays, *extra)


def attend_kernel(
    place_ref, picks_ref, own_hbm, other_hbm,
    first_hbm, mine_hbm, theirs_hbm,
    own_ref, other_ref, kt_ref, vt_ref, s0_ref, s1_ref, t0_ref, t1_ref, d_ref, low_ref, ds_ref,
    mine_ref, sum_ref, theirs_ref, first_ref, in_sem, first_sem, mine_sem, theirs_sem,
):
    nb = picks_ref.shape[0]
    half_at, seg = place_ref[0], place_ref[1]
    scale = 1.0 / math.sqrt(HD)
    power = scale * math.log2(math.e)
    s_refs, t_refs = (s0_ref, s1_ref), (t0_ref, t1_ref)
    chunks = [(j, half) for half in range(2) for j in range(TOPK + 1)]
    rows = [pl.ds(n * ROWS, ROWS) for n in range(len(chunks))]

    def loads(b):
        at = pl.ds(b * PART, PART)
        return (
            pltpu.make_async_copy(own_hbm.at[at], own_ref.at[at], in_sem.at[b, 0]),
            pltpu.make_async_copy(other_hbm.at[at], other_ref.at[at], in_sem.at[b, 1]),
        )

    def start(b, carry):
        for copy in loads(b):
            copy.start()
        return carry

    def arrive(b):
        for copy in loads(b):
            copy.wait()

    def part(a, half, b):
        ref = own_ref if half == 0 else other_ref
        return ref[pl.ds(b * PART, PART), a].reshape(ROWS, HD)

    def slots_of(i):
        return [picks_ref[i, j] for j in range(TOPK)] + [i]

    def turn(b):
        for half in range(2):
            kt_ref[half * nb + b] = part(0, half, b).T
            vt_ref[half * nb + b] = part(1, half, b).T

    def scores(i, buf):
        qt = part(2, 0, i).T
        slots = slots_of(i)
        key_at = lax.broadcasted_iota(jnp.int32, (ROWS, ROWS), 0)
        query_at = lax.broadcasted_iota(jnp.int32, (ROWS, ROWS), 1)
        top = jnp.full((8, ROWS), -jnp.inf, F32)
        for n, (j, half) in enumerate(chunks):
            s = dot(part(0, half, slots[j]), qt)
            if j < TOPK:
                valid = slots[j] < i
            elif half == 0:
                valid = key_at <= query_at
            else:
                valid = key_at // HALF < query_at // HALF + half_at
            s = jnp.where(valid, s, -jnp.inf)
            s_refs[buf][rows[n]] = s
            top = jnp.maximum(top, jnp.max(s.reshape(ROWS // 8, 8, ROWS), axis=0))
        t_refs[buf][...] = jnp.broadcast_to(jnp.max(top, axis=0, keepdims=True), (8, ROWS))

    def add_terms(a, terms, slots):
        for n, (j, half) in enumerate(chunks):
            acc = mine_ref if half == 0 else sum_ref
            at = pl.ds(slots[j] * PART, PART)
            term = terms[n * ROWS : (n + 1) * ROWS].reshape(PART, HALF, HD)
            if j < TOPK:
                acc[a, at] += term
            else:
                acc[a, at] = term

    def flat(ref, slots):
        return jnp.concatenate([ref[half * nb + slots[j]] for j, half in chunks], axis=1)

    def rest(i, buf):
        s_ref = s_refs[buf]
        q, g = part(2, 0, i), part(3, 0, i)
        gt = g.T
        slots = slots_of(i)
        top = t_refs[buf][...]
        total = jnp.zeros((8, ROWS), F32)
        for n in range(len(chunks)):
            e = jnp.exp2((s_ref[rows[n]].reshape(ROWS // 8, 8, ROWS) - top) * power)
            s_ref[rows[n]] = e.reshape(ROWS, ROWS)
            total = total + jnp.sum(e, axis=0)
        t_refs[buf][...] = jnp.broadcast_to(1.0 / jnp.sum(total, axis=0, keepdims=True), (8, ROWS))
        inverse = t_refs[buf][...]
        for n in range(len(chunks)):
            low = s_ref[rows[n]].reshape(ROWS // 8, 8, ROWS) * inverse
            low_ref[rows[n]] = low.reshape(ROWS, ROWS).astype(BF)
        out_t = dot(flat(vt_ref, slots), low_ref[...])
        add_terms(1, dot(low_ref[...], g), slots)
        out = out_t.T.astype(BF)
        delta = jnp.sum(gt.astype(F32) * out_t.astype(BF).astype(F32), axis=0, keepdims=True)
        d_ref[...] = jnp.broadcast_to(delta, (8, ROWS))
        delta = d_ref[...]
        for n, (j, half) in enumerate(chunks):
            dp = dot(part(1, half, slots[j]), gt).reshape(ROWS // 8, 8, ROWS)
            ds = s_ref[rows[n]].reshape(ROWS // 8, 8, ROWS) * inverse * (dp - delta)
            ds_ref[rows[n]] = ds.reshape(ROWS, ROWS).astype(BF)
        query_t = dot(flat(kt_ref, slots), ds_ref[...])
        add_terms(0, dot(ds_ref[...], q), slots)
        query = (query_t * scale).T.astype(BF)
        first = jnp.where(seg == 0, out.astype(F32), query.astype(F32)).astype(BF)
        first_ref[pl.ds(i * PART, PART)] = first.reshape(PART, HALF, HD)

    def send_first(p):
        at = pl.ds(p * 2 * PART, 2 * PART)
        return pltpu.make_async_copy(first_ref.at[at], first_hbm.at[at, 0], first_sem.at[p])

    lax.fori_loop(0, nb, start, 0)
    arrive(0)
    turn(0)
    scores(0, 0)

    def pair(p, carry):
        i = 2 * p
        later = jnp.minimum(i + 2, nb - 1)
        arrive(i + 1)

        @pl.when(i + 2 < nb)
        def _():
            arrive(i + 2)

        turn(i + 1)
        turn(later)
        scores(i + 1, 1)
        rest(i, 0)
        scores(later, 0)
        rest(i + 1, 1)
        send_first(p).start()
        return carry

    lax.fori_loop(0, nb // 2, pair, 0)

    def send_mine(a):
        return pltpu.make_async_copy(mine_ref.at[a], mine_hbm.at[a], mine_sem.at[a])

    def send_theirs(b):
        at = pl.ds(b * 4 * PART, 4 * PART)
        return pltpu.make_async_copy(theirs_ref.at[:, at], theirs_hbm.at[:, at], theirs_sem.at[b])

    for a in range(2):
        send_mine(a).start()
    for b in range(nb // 4):
        at = pl.ds(b * 4 * PART, 4 * PART)
        for a in range(2):
            theirs_ref[a, at] = sum_ref[a, at].astype(BF)
        send_theirs(b).start()
    for p in range(nb // 2):
        send_first(p).wait()
    for a in range(2):
        send_mine(a).wait()
    for b in range(nb // 4):
        send_theirs(b).wait()


def attend(place, picks, own, other):
    nb = picks.shape[0]
    n = nb * PART
    work = 6 * 2 * nb * ROWS * KEYS * HD
    return call(
        attend_kernel, "attend_head",
        [
            jax.ShapeDtypeStruct((n, 3, HALF, HD), BF),
            jax.ShapeDtypeStruct((2, n, HALF, HD), F32),
            jax.ShapeDtypeStruct((2, n, HALF, HD), BF),
        ],
        2, 2,
        [
            pltpu.VMEM((n, 4, HALF, HD), BF),
            pltpu.VMEM((n, 2, HALF, HD), BF),
            pltpu.VMEM((2 * nb, HD, ROWS), BF),
            pltpu.VMEM((2 * nb, HD, ROWS), BF),
            pltpu.VMEM((KEYS, ROWS), F32),
            pltpu.VMEM((KEYS, ROWS), F32),
            pltpu.VMEM((8, ROWS), F32),
            pltpu.VMEM((8, ROWS), F32),
            pltpu.VMEM((8, ROWS), F32),
            pltpu.VMEM((KEYS, ROWS), BF),
            pltpu.VMEM((KEYS, ROWS), BF),
            pltpu.VMEM((2, n, HALF, HD), F32),
            pltpu.VMEM((2, n, HALF, HD), F32),
            pltpu.VMEM((2, n, HALF, HD), BF),
            pltpu.VMEM((n, HALF, HD), BF),
            pltpu.SemaphoreType.DMA((nb, 2)),
            pltpu.SemaphoreType.DMA((nb // 2,)),
            pltpu.SemaphoreType.DMA((2,)),
            pltpu.SemaphoreType.DMA((nb // 4,)),
        ],
        42, 16 << 20, work,
    )(place, picks, own, other)


def combine(whole, mine, got):
    n = whole.shape[0]
    groups = 4
    size = n // groups

    def kernel(whole_ref, mine_hbm, got_hbm, out_hbm, mine_ref, got_ref, out_ref, in_sem, out_sem):
        scale = 1.0 / math.sqrt(HD)
        at = [pl.ds(g * size, size) for g in range(groups)]

        def loads(g):
            return (
                pltpu.make_async_copy(mine_hbm.at[:, at[g]], mine_ref.at[:, at[g]], in_sem.at[g, 0]),
                pltpu.make_async_copy(got_hbm.at[:, at[g]], got_ref.at[:, at[g]], in_sem.at[g, 1]),
            )

        def store(g):
            return pltpu.make_async_copy(out_ref.at[at[g]], out_hbm.at[at[g], 1:3], out_sem.at[g])

        for g in range(groups):
            for copy in loads(g):
                copy.start()
        for g in range(groups):
            for copy in loads(g):
                copy.wait()
            for a in range(2):
                value = mine_ref[a, at[g]] + got_ref[a, at[g]].astype(F32)
                out_ref[at[g], a] = (value * scale if a == 0 else value).astype(BF)
            store(g).start()
        for g in range(groups):
            store(g).wait()

    return call(
        kernel, "combine_halves", jax.ShapeDtypeStruct(whole.shape, BF), 0, 3,
        [
            pltpu.VMEM((2, n, HALF, HD), F32),
            pltpu.VMEM((2, n, HALF, HD), BF),
            pltpu.VMEM((n, 2, HALF, HD), BF),
            pltpu.SemaphoreType.DMA((groups, 2)),
            pltpu.SemaphoreType.DMA((groups,)),
        ],
        12, 8 << 20, aliases={0: 0},
    )(whole, mine, got)


def gather(core, source, base, high, results=None):
    heads = 4 * GROUP
    groups = heads // GROUP
    rows = slice(HALF, 2 * HALF) if high else slice(0, HALF)

    def kernel(place_ref, source_ref, *refs):
        outs = refs[-8:-4]
        got, cut, in_sem, out_sem = refs[-4:]

        def load(g):
            at = pl.ds(place_ref[1] + g * GROUP, GROUP)
            return pltpu.make_async_copy(source_ref.at[at], got.at[g], in_sem.at[g])

        def store(g, a):
            cols = pl.ds(g * GROUP * HD, GROUP * HD)
            return pltpu.make_async_copy(cut.at[g, a], outs[a].at[0, rows, cols], out_sem.at[g, a])

        for g in range(groups):
            load(g).start()
        for g in range(groups):
            load(g).wait()
            for a in range(4):
                live = place_ref[0] == (1 if a == 0 else 0)
                for h in range(GROUP):
                    value = got[g, h, max(a - 1, 0)]
                    cut[g, a, :, h * HD : (h + 1) * HD] = jnp.where(live, value, jnp.zeros_like(value))
                store(g, a).start()
        for g in range(groups):
            for a in range(4):
                store(g, a).wait()

    extra = [] if results is None else list(results)
    return call(
        kernel, "gather_heads", [jax.ShapeDtypeStruct((1, 2 * HALF, heads * HD), BF)] * 4, 1, 1 + len(extra),
        [
            pltpu.VMEM((groups, GROUP, 3, HALF, HD), BF),
            pltpu.VMEM((groups, 4, HALF, GROUP * HD), BF),
            pltpu.SemaphoreType.DMA((groups,)),
            pltpu.SemaphoreType.DMA((groups, 4)),
        ],
        8, 4 << 20, aliases={2 + a: a for a in range(4)} if extra else None,
    )(jnp.stack([core, base]), source, *extra)


def cut_out(name, out_shape, vmem, pieces, place, *sources, direct=False):
    def kernel(place_ref, *refs):
        out_ref, held, in_sem, out_sem = refs[-4:]
        first, then = [], []
        for n, (src, at) in enumerate(pieces(place_ref, refs[:-4])):
            if direct:
                first.append(pltpu.make_async_copy(src, out_ref.at[at], in_sem.at[n]))
            else:
                first.append(pltpu.make_async_copy(src, held.at[at], in_sem.at[n]))
                then.append(pltpu.make_async_copy(held.at[at], out_ref.at[at], out_sem.at[n]))
        for copy in first:
            copy.start()
        for n, copy in enumerate(first):
            copy.wait()
            if not direct:
                then[n].start()
        for copy in then:
            copy.wait()

    return call(
        kernel, name, jax.ShapeDtypeStruct(out_shape, BF), 1, len(sources),
        [pltpu.VMEM((8, HD) if direct else out_shape, BF), pltpu.SemaphoreType.DMA((4,)), pltpu.SemaphoreType.DMA((4,))],
        vmem, 2 << 20,
    )(place[None], *sources)


CHIPS = ("ctx", "tp")
SWAP = [(0, 1), (1, 0)]


def on_device(queries, keys, values, out_grad, chosen):
    heads = queries.shape[2] // HD
    core = lax.axis_index("pipe").astype(jnp.int32)
    seg = (lax.axis_index(CHIPS) // WIDE).astype(jnp.int32)

    place = jnp.stack([core ^ seg, seg])
    arrays = (keys, values, queries, out_grad)
    theirs = cut_out(
        "cut_tokens", (4, HALF, heads * HD), 56,
        lambda _, refs: [(ref.at[0, HALF : 2 * HALF], a) for a, ref in enumerate(refs)],
        core, *arrays,
    )
    got = lax.ppermute(theirs, "pipe", SWAP)
    other_chosen = lax.ppermute(chosen, "pipe", SWAP)
    parts = spread(core, [x[0] for x in arrays], core)
    parts = spread(core, [got], 1 - core, parts)
    picks = jnp.where(seg == core, chosen, other_chosen)[0]
    parts, picks, place = lax.optimization_barrier((parts, picks, place))

    own = lax.all_to_all(parts, CHIPS, 0, 0, tiled=True)
    n = own.shape[0]
    mine = cut_out(
        "cut_keys", (n, 2, HALF, HD), 50,
        lambda _, refs: [
            (refs[0].at[pl.ds(g * n // 4, n // 4), 0:2], pl.ds(g * n // 4, n // 4)) for g in range(4)
        ],
        core, own,
    )
    other = lax.ppermute(mine, "pipe", SWAP)
    first, mine, theirs = attend(place, picks, own, other)
    whole = combine(first, mine, lax.ppermute(theirs, "pipe", SWAP))

    back = lax.all_to_all(whole, CHIPS, 0, 0, tiled=True)
    theirs = cut_out(
        "cut_heads", (heads, 3, HALF, HD), 4,
        lambda place_ref, refs: [
            (refs[0].at[pl.ds(place_ref[0] * WIDE + g * GROUP, GROUP)], pl.ds(g * GROUP, GROUP)) for g in range(4)
        ],
        core, back, direct=True,
    )
    got = lax.ppermute(theirs, "pipe", SWAP)
    results = gather(core, back, (1 - core) * WIDE, True)
    return tuple(gather(core, got, core * 0, False, results))


def solution(mesh):
    placed = P("pipe", CHIPS, None)
    return jax.shard_map(
        on_device,
        mesh=mesh,
        in_specs=(placed,) * 4 + (P("pipe", None, None),),
        out_specs=(placed,) * 4,
        check_vma=False,
    )
```

```python
import math

import jax
import jax.numpy as jnp
from jax import lax
from jax.experimental import pallas as pl
from jax.experimental.pallas import tpu as pltpu
from jax.sharding import PartitionSpec as P

HD = 128
BLK = 512
TOPK = 3
HALF = 64
PART = 4
ROWS = PART * HALF
KEYS = 2 * (TOPK + 1) * ROWS
WIDE = 32
GROUP = 7
MIB = 1024 * 1024

BF = jnp.bfloat16
F32 = jnp.float32
NN = ((1,), (0,))
SMEM = pl.BlockSpec(memory_space=pltpu.SMEM)
ANY = pl.BlockSpec(memory_space=pl.ANY)


def dot(a, b):
    return lax.dot_general(a, b, (NN, ((), ())), preferred_element_type=F32)


def call(kernel, name, out_shape, n_smem, n_any, scratch, vmem, moved, flops=0, aliases=None):
    one = not isinstance(out_shape, list)
    return pl.pallas_call(
        kernel,
        in_specs=[SMEM] * n_smem + [ANY] * n_any,
        out_specs=ANY if one else [ANY] * len(out_shape),
        out_shape=out_shape,
        scratch_shapes=scratch,
        input_output_aliases=aliases or {},
        compiler_params=pltpu.CompilerParams(vmem_limit_bytes=vmem * MIB),
        cost_estimate=pl.CostEstimate(flops=flops, bytes_accessed=moved, transcendentals=0),
        name=name,
    )


def spread(core, arrays, base, whole=None):
    heads = arrays[0].shape[-1] // HD
    groups = heads // GROUP

    def kernel(place_ref, *refs):
        sources = refs[:4] if len(arrays) == 4 else [refs[0].at[a] for a in range(4)]
        out_ref, got, cut, in_sem, out_sem = refs[-5:]

        def load(g, a):
            return pltpu.make_async_copy(
                sources[a].at[0:HALF, pl.ds(g * GROUP * HD, GROUP * HD)], got.at[g, a], in_sem.at[g, a]
            )

        def store(g):
            at = pl.ds(place_ref[0] * WIDE + g * GROUP, GROUP)
            return pltpu.make_async_copy(cut.at[pl.ds(g * GROUP, GROUP)], out_ref.at[at], out_sem.at[g])

        for g in range(groups):
            for a in range(4):
                load(g, a).start()
        for g in range(groups):
            for a in range(4):
                load(g, a).wait()
                for h in range(GROUP):
                    cut[g * GROUP + h, a] = got[g, a, :, h * HD : (h + 1) * HD]
            store(g).start()
        for g in range(groups):
            store(g).wait()

    extra = [] if whole is None else [whole]
    return call(
        kernel, "spread_heads",
        jax.ShapeDtypeStruct((2 * WIDE, 4, HALF, HD), BF), 1, len(arrays) + len(extra),
        [
            pltpu.VMEM((groups, 4, HALF, GROUP * HD), BF),
            pltpu.VMEM((heads, 4, HALF, HD), BF),
            pltpu.SemaphoreType.DMA((groups, 4)),
            pltpu.SemaphoreType.DMA((groups,)),
        ],
        50 if extra else 56, 4 << 20, aliases={1 + len(arrays): 0} if extra else None,
    )(base[None], *arrays, *extra)


def attend_kernel(
    place_ref, picks_ref, own_hbm, other_hbm,
    first_hbm, mine_hbm, theirs_hbm,
    own_ref, other_ref, kt_ref, vt_ref, s0_ref, s1_ref, t0_ref, t1_ref, d_ref, low_ref, ds_ref,
    mine_ref, sum_ref, theirs_ref, first_ref, in_sem, first_sem, mine_sem, theirs_sem,
):
    nb = picks_ref.shape[0]
    half_at, seg = place_ref[0], place_ref[1]
    scale = 1.0 / math.sqrt(HD)
    power = scale * math.log2(math.e)
    s_refs, t_refs = (s0_ref, s1_ref), (t0_ref, t1_ref)
    chunks = [(j, half) for half in range(2) for j in range(TOPK + 1)]
    rows = [pl.ds(n * ROWS, ROWS) for n in range(len(chunks))]

    edges = (0, 1, 3, 9, nb)

    def loads(k):
        at = pl.ds(edges[k] * PART, (edges[k + 1] - edges[k]) * PART)
        return (
            pltpu.make_async_copy(own_hbm.at[at], own_ref.at[at], in_sem.at[k, 0]),
            pltpu.make_async_copy(other_hbm.at[at], other_ref.at[at], in_sem.at[k, 1]),
        )

    def arrive(k):
        for copy in loads(k):
            copy.wait()

    def part(a, half, b):
        ref = own_ref if half == 0 else other_ref
        return ref[pl.ds(b * PART, PART), a].reshape(ROWS, HD)

    def slots_of(i):
        return [picks_ref[i, j] for j in range(TOPK)] + [i]

    def turn(b):
        for half in range(2):
            kt_ref[half * nb + b] = part(0, half, b).T
            vt_ref[half * nb + b] = part(1, half, b).T

    def scores(i, buf):
        qt = part(2, 0, i).T
        slots = slots_of(i)
        key_at = lax.broadcasted_iota(jnp.int32, (ROWS, ROWS), 0)
        query_at = lax.broadcasted_iota(jnp.int32, (ROWS, ROWS), 1)
        top = jnp.full((8, ROWS), -jnp.inf, F32)
        for n, (j, half) in enumerate(chunks):
            s = dot(part(0, half, slots[j]), qt)
            if j < TOPK:
                valid = slots[j] < i
            elif half == 0:
                valid = key_at <= query_at
            else:
                valid = key_at // HALF < query_at // HALF + half_at
            s = jnp.where(valid, s, -jnp.inf)
            s_refs[buf][rows[n]] = s
            top = jnp.maximum(top, jnp.max(s.reshape(ROWS // 8, 8, ROWS), axis=0))
        t_refs[buf][...] = jnp.broadcast_to(jnp.max(top, axis=0, keepdims=True), (8, ROWS))

    def add_terms(a, terms, slots):
        for n, (j, half) in enumerate(chunks):
            acc = mine_ref if half == 0 else sum_ref
            at = pl.ds(slots[j] * PART, PART)
            term = terms[n * ROWS : (n + 1) * ROWS].reshape(PART, HALF, HD)
            if j < TOPK:
                acc[a, at] += term
            else:
                acc[a, at] = term

    def flat(ref, slots):
        return jnp.concatenate([ref[half * nb + slots[j]] for j, half in chunks], axis=1)

    def rest(i, buf):
        s_ref = s_refs[buf]
        q, g = part(2, 0, i), part(3, 0, i)
        gt = g.T
        slots = slots_of(i)
        top = t_refs[buf][...]
        total = jnp.zeros((8, ROWS), F32)
        for n in range(len(chunks)):
            e = jnp.exp2((s_ref[rows[n]].reshape(ROWS // 8, 8, ROWS) - top) * power)
            s_ref[rows[n]] = e.reshape(ROWS, ROWS)
            total = total + jnp.sum(e, axis=0)
        t_refs[buf][...] = jnp.broadcast_to(1.0 / jnp.sum(total, axis=0, keepdims=True), (8, ROWS))
        inverse = t_refs[buf][...]
        for n in range(len(chunks)):
            low = s_ref[rows[n]].reshape(ROWS // 8, 8, ROWS) * inverse
            low_ref[rows[n]] = low.reshape(ROWS, ROWS).astype(BF)
        out_t = dot(flat(vt_ref, slots), low_ref[...])
        add_terms(1, dot(low_ref[...], g), slots)
        out = out_t.astype(BF).T
        delta = jnp.sum(gt.astype(F32) * out_t.astype(BF).astype(F32), axis=0, keepdims=True)
        d_ref[...] = jnp.broadcast_to(delta, (8, ROWS))
        delta = d_ref[...]
        for n, (j, half) in enumerate(chunks):
            dp = dot(part(1, half, slots[j]), gt).reshape(ROWS // 8, 8, ROWS)
            ds = s_ref[rows[n]].reshape(ROWS // 8, 8, ROWS) * inverse * (dp - delta)
            ds_ref[rows[n]] = ds.reshape(ROWS, ROWS).astype(BF)
        query_t = dot(flat(kt_ref, slots), ds_ref[...])
        add_terms(0, dot(ds_ref[...], q), slots)
        query = (query_t * scale).astype(BF).T
        first = jnp.where(seg == 0, out.astype(F32), query.astype(F32)).astype(BF)
        first_ref[pl.ds(i * PART, PART)] = first.reshape(PART, HALF, HD)

    def send_first(p):
        at = pl.ds(p * 2 * PART, 2 * PART)
        return pltpu.make_async_copy(first_ref.at[at], first_hbm.at[at, 0], first_sem.at[p])

    for k in range(len(edges) - 1):
        for copy in loads(k):
            copy.start()
    arrive(0)
    turn(0)
    scores(0, 0)

    def pair(p, carry):
        i = 2 * p
        later = jnp.minimum(i + 2, nb - 1)

        for k in range(1, len(edges) - 1):

            @pl.when(i + 1 == edges[k])
            def _(k=k):
                arrive(k)

        turn(i + 1)
        turn(later)
        scores(i + 1, 1)
        rest(i, 0)
        scores(later, 0)
        rest(i + 1, 1)
        send_first(p).start()
        return carry

    lax.fori_loop(0, nb // 2, pair, 0)

    def send_mine(a):
        return pltpu.make_async_copy(mine_ref.at[a], mine_hbm.at[a], mine_sem.at[a])

    def send_theirs(b):
        at = pl.ds(b * 4 * PART, 4 * PART)
        return pltpu.make_async_copy(theirs_ref.at[:, at], theirs_hbm.at[:, at], theirs_sem.at[b])

    for a in range(2):
        send_mine(a).start()
    for b in range(nb // 4):
        at = pl.ds(b * 4 * PART, 4 * PART)
        for a in range(2):
            theirs_ref[a, at] = sum_ref[a, at].astype(BF)
        send_theirs(b).start()
    for p in range(nb // 2):
        send_first(p).wait()
    for a in range(2):
        send_mine(a).wait()
    for b in range(nb // 4):
        send_theirs(b).wait()


def attend(place, picks, own, other):
    nb = picks.shape[0]
    n = nb * PART
    work = 6 * 2 * nb * ROWS * KEYS * HD
    return call(
        attend_kernel, "attend_head",
        [
            jax.ShapeDtypeStruct((n, 3, HALF, HD), BF),
            jax.ShapeDtypeStruct((2, n, HALF, HD), F32),
            jax.ShapeDtypeStruct((2, n, HALF, HD), BF),
        ],
        2, 2,
        [
            pltpu.VMEM((n, 4, HALF, HD), BF),
            pltpu.VMEM((n, 2, HALF, HD), BF),
            pltpu.VMEM((2 * nb, HD, ROWS), BF),
            pltpu.VMEM((2 * nb, HD, ROWS), BF),
            pltpu.VMEM((KEYS, ROWS), F32),
            pltpu.VMEM((KEYS, ROWS), F32),
            pltpu.VMEM((8, ROWS), F32),
            pltpu.VMEM((8, ROWS), F32),
            pltpu.VMEM((8, ROWS), F32),
            pltpu.VMEM((KEYS, ROWS), BF),
            pltpu.VMEM((KEYS, ROWS), BF),
            pltpu.VMEM((2, n, HALF, HD), F32),
            pltpu.VMEM((2, n, HALF, HD), F32),
            pltpu.VMEM((2, n, HALF, HD), BF),
            pltpu.VMEM((n, HALF, HD), BF),
            pltpu.SemaphoreType.DMA((4, 2)),
            pltpu.SemaphoreType.DMA((nb // 2,)),
            pltpu.SemaphoreType.DMA((2,)),
            pltpu.SemaphoreType.DMA((nb // 4,)),
        ],
        42, 16 << 20, work,
    )(place, picks, own, other)


def combine(whole, mine, got):
    n = whole.shape[0]
    groups = 4
    size = n // groups

    def kernel(whole_ref, mine_hbm, got_hbm, out_hbm, mine_ref, got_ref, out_ref, in_sem, out_sem):
        scale = 1.0 / math.sqrt(HD)
        at = [pl.ds(g * size, size) for g in range(groups)]

        def loads(g):
            return (
                pltpu.make_async_copy(mine_hbm.at[:, at[g]], mine_ref.at[:, at[g]], in_sem.at[g, 0]),
                pltpu.make_async_copy(got_hbm.at[:, at[g]], got_ref.at[:, at[g]], in_sem.at[g, 1]),
            )

        def store(g):
            return pltpu.make_async_copy(out_ref.at[at[g]], out_hbm.at[at[g], 1:3], out_sem.at[g])

        for g in range(groups):
            for copy in loads(g):
                copy.start()
        for g in range(groups):
            for copy in loads(g):
                copy.wait()
            for a in range(2):
                value = mine_ref[a, at[g]] + got_ref[a, at[g]].astype(F32)
                out_ref[at[g], a] = (value * scale if a == 0 else value).astype(BF)
            store(g).start()
        for g in range(groups):
            store(g).wait()

    return call(
        kernel, "combine_halves", jax.ShapeDtypeStruct(whole.shape, BF), 0, 3,
        [
            pltpu.VMEM((2, n, HALF, HD), F32),
            pltpu.VMEM((2, n, HALF, HD), BF),
            pltpu.VMEM((n, 2, HALF, HD), BF),
            pltpu.SemaphoreType.DMA((groups, 2)),
            pltpu.SemaphoreType.DMA((groups,)),
        ],
        12, 8 << 20, aliases={0: 0},
    )(whole, mine, got)


def gather(core, source, base, high, results=None):
    heads = 4 * GROUP
    groups = heads // GROUP
    rows = slice(HALF, 2 * HALF) if high else slice(0, HALF)

    def kernel(place_ref, source_ref, *refs):
        outs = refs[-8:-4]
        got, cut, in_sem, out_sem = refs[-4:]

        def load(g):
            at = pl.ds(place_ref[1] + g * GROUP, GROUP)
            return pltpu.make_async_copy(source_ref.at[at], got.at[g], in_sem.at[g])

        def store(g, a):
            cols = pl.ds(g * GROUP * HD, GROUP * HD)
            return pltpu.make_async_copy(cut.at[g, a], outs[a].at[0, rows, cols], out_sem.at[g, a])

        for g in range(groups):
            load(g).start()
        for g in range(groups):
            load(g).wait()
            for a in range(4):
                live = place_ref[0] == (1 if a == 0 else 0)
                for h in range(GROUP):
                    value = got[g, h, max(a - 1, 0)]
                    cut[g, a, :, h * HD : (h + 1) * HD] = jnp.where(live, value, jnp.zeros_like(value))
                store(g, a).start()
        for g in range(groups):
            for a in range(4):
                store(g, a).wait()

    extra = [] if results is None else list(results)
    return call(
        kernel, "gather_heads", [jax.ShapeDtypeStruct((1, 2 * HALF, heads * HD), BF)] * 4, 1, 1 + len(extra),
        [
            pltpu.VMEM((groups, GROUP, 3, HALF, HD), BF),
            pltpu.VMEM((groups, 4, HALF, GROUP * HD), BF),
            pltpu.SemaphoreType.DMA((groups,)),
            pltpu.SemaphoreType.DMA((groups, 4)),
        ],
        8, 4 << 20, aliases={2 + a: a for a in range(4)} if extra else None,
    )(jnp.stack([core, base]), source, *extra)


def cut_out(name, out_shape, vmem, pieces, place, *sources, direct=False):
    def kernel(place_ref, *refs):
        out_ref, held, in_sem, out_sem = refs[-4:]
        first, then = [], []
        for n, (src, at) in enumerate(pieces(place_ref, refs[:-4])):
            if direct:
                first.append(pltpu.make_async_copy(src, out_ref.at[at], in_sem.at[n]))
            else:
                first.append(pltpu.make_async_copy(src, held.at[at], in_sem.at[n]))
                then.append(pltpu.make_async_copy(held.at[at], out_ref.at[at], out_sem.at[n]))
        for copy in first:
            copy.start()
        for n, copy in enumerate(first):
            copy.wait()
            if not direct:
                then[n].start()
        for copy in then:
            copy.wait()

    return call(
        kernel, name, jax.ShapeDtypeStruct(out_shape, BF), 1, len(sources),
        [pltpu.VMEM((8, HD) if direct else out_shape, BF), pltpu.SemaphoreType.DMA((4,)), pltpu.SemaphoreType.DMA((4,))],
        vmem, 2 << 20,
    )(place[None], *sources)


CHIPS = ("ctx", "tp")
SWAP = [(0, 1), (1, 0)]


def on_device(queries, keys, values, out_grad, chosen):
    heads = queries.shape[2] // HD
    core = lax.axis_index("pipe").astype(jnp.int32)
    seg = (lax.axis_index(CHIPS) // WIDE).astype(jnp.int32)

    place = jnp.stack([core ^ seg, seg])
    arrays = (keys, values, queries, out_grad)
    theirs = cut_out(
        "cut_tokens", (4, HALF, heads * HD), 56,
        lambda _, refs: [(ref.at[0, HALF : 2 * HALF], a) for a, ref in enumerate(refs)],
        core, *arrays,
    )
    got = lax.ppermute(theirs, "pipe", SWAP)
    other_chosen = lax.ppermute(chosen, "pipe", SWAP)
    parts = spread(core, [x[0] for x in arrays], core)
    parts = spread(core, [got], 1 - core, parts)
    parts, other_chosen = lax.optimization_barrier((parts, other_chosen))

    own = lax.all_to_all(parts, CHIPS, 0, 0, tiled=True)
    own, other_chosen = lax.optimization_barrier((own, other_chosen))
    picks = jnp.where(seg == core, chosen, other_chosen)[0]
    n = own.shape[0]
    mine = cut_out(
        "cut_keys", (n, 2, HALF, HD), 50,
        lambda _, refs: [
            (refs[0].at[pl.ds(g * n // 4, n // 4), 0:2], pl.ds(g * n // 4, n // 4)) for g in range(4)
        ],
        core, own,
    )
    other = lax.ppermute(mine, "pipe", SWAP)
    first, mine, theirs = attend(place, picks, own, other)
    whole = combine(first, mine, lax.ppermute(theirs, "pipe", SWAP))

    back = lax.all_to_all(whole, CHIPS, 0, 0, tiled=True)
    theirs = cut_out(
        "cut_heads", (heads, 3, HALF, HD), 4,
        lambda place_ref, refs: [
            (refs[0].at[pl.ds(place_ref[0] * WIDE + g * GROUP, GROUP)], pl.ds(g * GROUP, GROUP)) for g in range(4)
        ],
        core, back, direct=True,
    )
    got = lax.ppermute(theirs, "pipe", SWAP)
    results = gather(core, back, (1 - core) * WIDE, True)
    return tuple(gather(core, got, core * 0, False, results))


def solution(mesh):
    placed = P("pipe", CHIPS, None)
    return jax.shard_map(
        on_device,
        mesh=mesh,
        in_specs=(placed,) * 4 + (P("pipe", None, None),),
        out_specs=(placed,) * 4,
        check_vma=False,
    )
```

```python
import math

import jax
import jax.numpy as jnp
from jax import lax
from jax.experimental import pallas as pl
from jax.experimental.pallas import tpu as pltpu
from jax.sharding import PartitionSpec as P

HD = 128
BLK = 512
TOPK = 3
HALF = 64
PART = 4
ROWS = PART * HALF
KEYS = 2 * (TOPK + 1) * ROWS
WIDE = 32
GROUP = 7
MIB = 1024 * 1024

BF = jnp.bfloat16
F32 = jnp.float32
NN = ((1,), (0,))
SMEM = pl.BlockSpec(memory_space=pltpu.SMEM)
ANY = pl.BlockSpec(memory_space=pl.ANY)


def dot(a, b):
    return lax.dot_general(a, b, (NN, ((), ())), preferred_element_type=F32)


def call(kernel, name, out_shape, n_smem, n_any, scratch, vmem, moved, flops=0, aliases=None):
    one = not isinstance(out_shape, list)
    return pl.pallas_call(
        kernel,
        in_specs=[SMEM] * n_smem + [ANY] * n_any,
        out_specs=ANY if one else [ANY] * len(out_shape),
        out_shape=out_shape,
        scratch_shapes=scratch,
        input_output_aliases=aliases or {},
        compiler_params=pltpu.CompilerParams(vmem_limit_bytes=vmem * MIB),
        cost_estimate=pl.CostEstimate(flops=flops, bytes_accessed=moved, transcendentals=0),
        name=name,
    )


def spread(core, arrays, base, whole=None):
    heads = arrays[0].shape[-1] // HD
    groups = heads // GROUP

    def kernel(place_ref, *refs):
        sources = refs[:4] if len(arrays) == 4 else [refs[0].at[a] for a in range(4)]
        out_ref, got, cut, in_sem, out_sem = refs[-5:]

        def load(g, a):
            return pltpu.make_async_copy(
                sources[a].at[0:HALF, pl.ds(g * GROUP * HD, GROUP * HD)], got.at[g, a], in_sem.at[g, a]
            )

        def store(g):
            at = pl.ds(place_ref[0] * WIDE + g * GROUP, GROUP)
            return pltpu.make_async_copy(cut.at[pl.ds(g * GROUP, GROUP)], out_ref.at[at], out_sem.at[g])

        for g in range(groups):
            for a in range(4):
                load(g, a).start()
        for g in range(groups):
            for a in range(4):
                load(g, a).wait()
                for h in range(GROUP):
                    cut[g * GROUP + h, a] = got[g, a, :, h * HD : (h + 1) * HD]
            store(g).start()
        for g in range(groups):
            store(g).wait()

    extra = [] if whole is None else [whole]
    return call(
        kernel, "spread_heads",
        jax.ShapeDtypeStruct((2 * WIDE, 4, HALF, HD), BF), 1, len(arrays) + len(extra),
        [
            pltpu.VMEM((groups, 4, HALF, GROUP * HD), BF),
            pltpu.VMEM((heads, 4, HALF, HD), BF),
            pltpu.SemaphoreType.DMA((groups, 4)),
            pltpu.SemaphoreType.DMA((groups,)),
        ],
        50 if extra else 56, 4 << 20, aliases={1 + len(arrays): 0} if extra else None,
    )(base[None], *arrays, *extra)


def attend_kernel(
    place_ref, picks_ref, own_hbm, other_hbm,
    first_hbm, mine_hbm, theirs_hbm,
    own_ref, other_ref, kt_ref, vt_ref, s0_ref, s1_ref, t0_ref, t1_ref, d_ref, low_ref, ds_ref,
    mine_ref, sum_ref, theirs_ref, first_ref, in_sem, first_sem, mine_sem, theirs_sem,
):
    nb = picks_ref.shape[0]
    half_at, seg = place_ref[0], place_ref[1]
    scale = 1.0 / math.sqrt(HD)
    power = scale * math.log2(math.e)
    s_refs, t_refs = (s0_ref, s1_ref), (t0_ref, t1_ref)
    chunks = [(j, half) for half in range(2) for j in range(TOPK + 1)]
    rows = [pl.ds(n * ROWS, ROWS) for n in range(len(chunks))]

    edges = (0, 1, 3, 9, nb)

    def loads(k):
        at = pl.ds(edges[k] * PART, (edges[k + 1] - edges[k]) * PART)
        return (
            pltpu.make_async_copy(own_hbm.at[at], own_ref.at[at], in_sem.at[k, 0]),
            pltpu.make_async_copy(other_hbm.at[at], other_ref.at[at], in_sem.at[k, 1]),
        )

    def arrive(k):
        for copy in loads(k):
            copy.wait()

    def part(a, half, b):
        ref = own_ref if half == 0 else other_ref
        return ref[pl.ds(b * PART, PART), a].reshape(ROWS, HD)

    def slots_of(i):
        return [picks_ref[i, j] for j in range(TOPK)] + [i]

    def turn(b):
        for half in range(2):
            kt_ref[half * nb + b] = part(0, half, b).T
            vt_ref[half * nb + b] = part(1, half, b).T

    def scores(i, buf):
        qt = part(2, 0, i).T
        slots = slots_of(i)
        key_at = lax.broadcasted_iota(jnp.int32, (ROWS, ROWS), 0)
        query_at = lax.broadcasted_iota(jnp.int32, (ROWS, ROWS), 1)
        top = jnp.full((8, ROWS), -jnp.inf, F32)
        for n, (j, half) in enumerate(chunks):
            s = dot(part(0, half, slots[j]), qt)
            if j < TOPK:
                valid = slots[j] < i
            elif half == 0:
                valid = key_at <= query_at
            else:
                valid = key_at // HALF < query_at // HALF + half_at
            s = jnp.where(valid, s, -jnp.inf)
            s_refs[buf][rows[n]] = s
            top = jnp.maximum(top, jnp.max(s.reshape(ROWS // 8, 8, ROWS), axis=0))
        t_refs[buf][...] = jnp.broadcast_to(jnp.max(top, axis=0, keepdims=True), (8, ROWS))

    def add_terms(a, terms, slots):
        for n, (j, half) in enumerate(chunks):
            acc = mine_ref if half == 0 else sum_ref
            at = pl.ds(slots[j] * PART, PART)
            term = terms[n * ROWS : (n + 1) * ROWS].reshape(PART, HALF, HD)
            if j < TOPK:
                acc[a, at] += term
            else:
                acc[a, at] = term

    def flat(ref, slots):
        return jnp.concatenate([ref[half * nb + slots[j]] for j, half in chunks], axis=1)

    def rest(i, buf):
        s_ref = s_refs[buf]
        q, g = part(2, 0, i), part(3, 0, i)
        gt = g.T
        slots = slots_of(i)
        top = t_refs[buf][...]
        total = jnp.zeros((8, ROWS), F32)
        for n in range(len(chunks)):
            e = jnp.exp2((s_ref[rows[n]].reshape(ROWS // 8, 8, ROWS) - top) * power)
            s_ref[rows[n]] = e.reshape(ROWS, ROWS)
            total = total + jnp.sum(e, axis=0)
        t_refs[buf][...] = jnp.broadcast_to(1.0 / jnp.sum(total, axis=0, keepdims=True), (8, ROWS))
        inverse = t_refs[buf][...]
        for n in range(len(chunks)):
            low = s_ref[rows[n]].reshape(ROWS // 8, 8, ROWS) * inverse
            low_ref[rows[n]] = low.reshape(ROWS, ROWS).astype(BF)
        out_t = dot(flat(vt_ref, slots), low_ref[...])
        add_terms(1, dot(low_ref[...], g), slots)
        out = out_t.astype(BF).T
        delta = jnp.sum(gt.astype(F32) * out_t.astype(BF).astype(F32), axis=0, keepdims=True)
        d_ref[...] = jnp.broadcast_to(delta, (8, ROWS))
        delta = d_ref[...]
        for n, (j, half) in enumerate(chunks):
            dp = dot(part(1, half, slots[j]), gt).reshape(ROWS // 8, 8, ROWS)
            ds = s_ref[rows[n]].reshape(ROWS // 8, 8, ROWS) * inverse * (dp - delta)
            ds_ref[rows[n]] = ds.reshape(ROWS, ROWS).astype(BF)
        query_t = dot(flat(kt_ref, slots), ds_ref[...])
        add_terms(0, dot(ds_ref[...], q), slots)
        query = (query_t * scale).astype(BF).T
        first = jnp.where(seg == 0, out.astype(F32), query.astype(F32)).astype(BF)
        first_ref[pl.ds(i * PART, PART)] = first.reshape(PART, HALF, HD)

    def send_first(p):
        at = pl.ds(p * 2 * PART, 2 * PART)
        return pltpu.make_async_copy(first_ref.at[at], first_hbm.at[at, 0], first_sem.at[p])

    for k in range(len(edges) - 1):
        for copy in loads(k):
            copy.start()
    arrive(0)
    turn(0)
    scores(0, 0)

    def pair(p, carry):
        i = 2 * p
        later = jnp.minimum(i + 2, nb - 1)

        for k in range(1, len(edges) - 1):

            @pl.when(i + 1 == edges[k])
            def _(k=k):
                arrive(k)

        turn(i + 1)
        turn(later)
        scores(i + 1, 1)
        rest(i, 0)
        scores(later, 0)
        rest(i + 1, 1)
        send_first(p).start()
        return carry

    lax.fori_loop(0, nb // 2, pair, 0)

    def send_mine(a):
        return pltpu.make_async_copy(mine_ref.at[a], mine_hbm.at[a], mine_sem.at[a])

    def send_theirs(b):
        at = pl.ds(b * 4 * PART, 4 * PART)
        return pltpu.make_async_copy(theirs_ref.at[:, at], theirs_hbm.at[:, at], theirs_sem.at[b])

    for a in range(2):
        send_mine(a).start()
    for b in range(nb // 4):
        at = pl.ds(b * 4 * PART, 4 * PART)
        for a in range(2):
            theirs_ref[a, at] = sum_ref[a, at].astype(BF)
        send_theirs(b).start()
    for p in range(nb // 2):
        send_first(p).wait()
    for a in range(2):
        send_mine(a).wait()
    for b in range(nb // 4):
        send_theirs(b).wait()


def attend(place, picks, own, other):
    nb = picks.shape[0]
    n = nb * PART
    work = 6 * 2 * nb * ROWS * KEYS * HD
    return call(
        attend_kernel, "attend_head",
        [
            jax.ShapeDtypeStruct((n, 3, HALF, HD), BF),
            jax.ShapeDtypeStruct((2, n, HALF, HD), F32),
            jax.ShapeDtypeStruct((2, n, HALF, HD), BF),
        ],
        2, 2,
        [
            pltpu.VMEM((n, 4, HALF, HD), BF),
            pltpu.VMEM((n, 2, HALF, HD), BF),
            pltpu.VMEM((2 * nb, HD, ROWS), BF),
            pltpu.VMEM((2 * nb, HD, ROWS), BF),
            pltpu.VMEM((KEYS, ROWS), F32),
            pltpu.VMEM((KEYS, ROWS), F32),
            pltpu.VMEM((8, ROWS), F32),
            pltpu.VMEM((8, ROWS), F32),
            pltpu.VMEM((8, ROWS), F32),
            pltpu.VMEM((KEYS, ROWS), BF),
            pltpu.VMEM((KEYS, ROWS), BF),
            pltpu.VMEM((2, n, HALF, HD), F32),
            pltpu.VMEM((2, n, HALF, HD), F32),
            pltpu.VMEM((2, n, HALF, HD), BF),
            pltpu.VMEM((n, HALF, HD), BF),
            pltpu.SemaphoreType.DMA((4, 2)),
            pltpu.SemaphoreType.DMA((nb // 2,)),
            pltpu.SemaphoreType.DMA((2,)),
            pltpu.SemaphoreType.DMA((nb // 4,)),
        ],
        42, 16 << 20, work,
    )(place, picks, own, other)


def combine(whole, mine, got):
    n = whole.shape[0]
    groups = 4
    size = n // groups

    def kernel(whole_ref, mine_hbm, got_hbm, out_hbm, mine_ref, got_ref, out_ref, in_sem, out_sem):
        scale = 1.0 / math.sqrt(HD)
        at = [pl.ds(g * size, size) for g in range(groups)]

        def loads(g):
            return (
                pltpu.make_async_copy(mine_hbm.at[:, at[g]], mine_ref.at[:, at[g]], in_sem.at[g, 0]),
                pltpu.make_async_copy(got_hbm.at[:, at[g]], got_ref.at[:, at[g]], in_sem.at[g, 1]),
            )

        def store(g):
            return pltpu.make_async_copy(out_ref.at[at[g]], out_hbm.at[at[g], 1:3], out_sem.at[g])

        for g in range(groups):
            for copy in loads(g):
                copy.start()
        for g in range(groups):
            for copy in loads(g):
                copy.wait()
            for a in range(2):
                value = mine_ref[a, at[g]] + got_ref[a, at[g]].astype(F32)
                out_ref[at[g], a] = (value * scale if a == 0 else value).astype(BF)
            store(g).start()
        for g in range(groups):
            store(g).wait()

    return call(
        kernel, "combine_halves", jax.ShapeDtypeStruct(whole.shape, BF), 0, 3,
        [
            pltpu.VMEM((2, n, HALF, HD), F32),
            pltpu.VMEM((2, n, HALF, HD), BF),
            pltpu.VMEM((n, 2, HALF, HD), BF),
            pltpu.SemaphoreType.DMA((groups, 2)),
            pltpu.SemaphoreType.DMA((groups,)),
        ],
        12, 8 << 20, aliases={0: 0},
    )(whole, mine, got)


def gather(core, source, base, high, results=None):
    heads = 4 * GROUP
    groups = heads // GROUP
    rows = slice(HALF, 2 * HALF) if high else slice(0, HALF)

    def kernel(place_ref, source_ref, *refs):
        outs = refs[-10:-6]
        got, cut, blank, in_sem, out_sem, blank_sem = refs[-6:]
        live = [place_ref[0] == (1 if a == 0 else 0) for a in range(4)]

        def clear(a):
            return pltpu.make_async_copy(blank, outs[a].at[0, 0:HALF], blank_sem.at[a])

        def fill(g, a):
            for h in range(GROUP):
                value = got[g, h, max(a - 1, 0)]
                if high:
                    value = jnp.where(live[a], value, jnp.zeros_like(value))
                cut[g, a, :, h * HD : (h + 1) * HD] = value
            store(g, a).start()

        def load(g):
            at = pl.ds(place_ref[1] + g * GROUP, GROUP)
            return pltpu.make_async_copy(source_ref.at[at], got.at[g], in_sem.at[g])

        def store(g, a):
            cols = pl.ds(g * GROUP * HD, GROUP * HD)
            return pltpu.make_async_copy(cut.at[g, a], outs[a].at[0, rows, cols], out_sem.at[g, a])

        for g in range(groups):
            load(g).start()
        for g in range(groups):
            load(g).wait()
            for a in range(4):
                if high:
                    fill(g, a)
                else:
                    pl.when(live[a])(lambda g=g, a=a: fill(g, a))
        if high:
            blank[...] = jnp.zeros_like(blank)
            for a in range(4):
                pl.when(jnp.logical_not(live[a]))(lambda a=a: clear(a).start())
        for a in range(4):
            if high:
                for g in range(groups):
                    store(g, a).wait()
                pl.when(jnp.logical_not(live[a]))(lambda a=a: clear(a).wait())
            else:
                pl.when(live[a])(lambda a=a: [store(g, a).wait() for g in range(groups)] and None)

    extra = [] if results is None else list(results)
    return call(
        kernel, "gather_heads", [jax.ShapeDtypeStruct((1, 2 * HALF, heads * HD), BF)] * 4, 1, 1 + len(extra),
        [
            pltpu.VMEM((groups, GROUP, 3, HALF, HD), BF),
            pltpu.VMEM((groups, 4, HALF, GROUP * HD), BF),
            pltpu.VMEM((HALF, heads * HD), BF),
            pltpu.SemaphoreType.DMA((groups,)),
            pltpu.SemaphoreType.DMA((groups, 4)),
            pltpu.SemaphoreType.DMA((4,)),
        ],
        8, 4 << 20, aliases={2 + a: a for a in range(4)} if extra else None,
    )(jnp.stack([core, base]), source, *extra)


def cut_out(name, out_shape, vmem, pieces, place, *sources, direct=False):
    def kernel(place_ref, *refs):
        out_ref, held, in_sem, out_sem = refs[-4:]
        first, then = [], []
        for n, (src, at) in enumerate(pieces(place_ref, refs[:-4])):
            if direct:
                first.append(pltpu.make_async_copy(src, out_ref.at[at], in_sem.at[n]))
            else:
                first.append(pltpu.make_async_copy(src, held.at[at], in_sem.at[n]))
                then.append(pltpu.make_async_copy(held.at[at], out_ref.at[at], out_sem.at[n]))
        for copy in first:
            copy.start()
        for n, copy in enumerate(first):
            copy.wait()
            if not direct:
                then[n].start()
        for copy in then:
            copy.wait()

    return call(
        kernel, name, jax.ShapeDtypeStruct(out_shape, BF), 1, len(sources),
        [pltpu.VMEM((8, HD) if direct else out_shape, BF), pltpu.SemaphoreType.DMA((4,)), pltpu.SemaphoreType.DMA((4,))],
        vmem, 2 << 20,
    )(place[None], *sources)


CHIPS = ("ctx", "tp")
SWAP = [(0, 1), (1, 0)]


def on_device(queries, keys, values, out_grad, chosen):
    heads = queries.shape[2] // HD
    core = lax.axis_index("pipe").astype(jnp.int32)
    seg = (lax.axis_index(CHIPS) // WIDE).astype(jnp.int32)

    place = jnp.stack([core ^ seg, seg])
    arrays = (keys, values, queries, out_grad)
    theirs = cut_out(
        "cut_tokens", (4, HALF, heads * HD), 56,
        lambda _, refs: [(ref.at[0, HALF : 2 * HALF], a) for a, ref in enumerate(refs)],
        core, *arrays,
    )
    got = lax.ppermute(theirs, "pipe", SWAP)
    other_chosen = lax.ppermute(chosen, "pipe", SWAP)
    parts = spread(core, [x[0] for x in arrays], core)
    parts = spread(core, [got], 1 - core, parts)
    parts, other_chosen = lax.optimization_barrier((parts, other_chosen))

    own = lax.all_to_all(parts, CHIPS, 0, 0, tiled=True)
    own, other_chosen = lax.optimization_barrier((own, other_chosen))
    picks = jnp.where(seg == core, chosen, other_chosen)[0]
    n = own.shape[0]
    mine = cut_out(
        "cut_keys", (n, 2, HALF, HD), 50,
        lambda _, refs: [
            (refs[0].at[pl.ds(g * n // 4, n // 4), 0:2], pl.ds(g * n // 4, n // 4)) for g in range(4)
        ],
        core, own,
    )
    other = lax.ppermute(mine, "pipe", SWAP)
    first, mine, theirs = attend(place, picks, own, other)
    whole = combine(first, mine, lax.ppermute(theirs, "pipe", SWAP))

    back = lax.all_to_all(whole, CHIPS, 0, 0, tiled=True)
    theirs = cut_out(
        "cut_heads", (heads, 3, HALF, HD), 4,
        lambda place_ref, refs: [
            (refs[0].at[pl.ds(place_ref[0] * WIDE + g * GROUP, GROUP)], pl.ds(g * GROUP, GROUP)) for g in range(4)
        ],
        core, back, direct=True,
    )
    got = lax.ppermute(theirs, "pipe", SWAP)
    results = gather(core, back, (1 - core) * WIDE, True)
    return tuple(gather(core, got, core * 0, False, results))


def solution(mesh):
    placed = P("pipe", CHIPS, None)
    return jax.shard_map(
        on_device,
        mesh=mesh,
        in_specs=(placed,) * 4 + (P("pipe", None, None),),
        out_specs=(placed,) * 4,
        check_vma=False,
    )
```

```python
import math

import jax
import jax.numpy as jnp
from jax import lax
from jax.experimental import pallas as pl
from jax.experimental.pallas import tpu as pltpu
from jax.sharding import PartitionSpec as P

HD = 128
BLK = 512
TOPK = 3
HALF = 64
PART = 4
ROWS = PART * HALF
KEYS = 2 * (TOPK + 1) * ROWS
WIDE = 32
GROUP = 7
MIB = 1024 * 1024

BF = jnp.bfloat16
F32 = jnp.float32
NN = ((1,), (0,))
SMEM = pl.BlockSpec(memory_space=pltpu.SMEM)
ANY = pl.BlockSpec(memory_space=pl.ANY)


def dot(a, b):
    return lax.dot_general(a, b, (NN, ((), ())), preferred_element_type=F32)


def call(kernel, name, out_shape, n_smem, n_any, scratch, vmem, moved, flops=0, aliases=None):
    one = not isinstance(out_shape, list)
    return pl.pallas_call(
        kernel,
        in_specs=[SMEM] * n_smem + [ANY] * n_any,
        out_specs=ANY if one else [ANY] * len(out_shape),
        out_shape=out_shape,
        scratch_shapes=scratch,
        input_output_aliases=aliases or {},
        compiler_params=pltpu.CompilerParams(vmem_limit_bytes=vmem * MIB),
        cost_estimate=pl.CostEstimate(flops=flops, bytes_accessed=moved, transcendentals=0),
        name=name,
    )


def spread(core, arrays, base, whole=None):
    heads = arrays[0].shape[-1] // HD
    groups = heads // GROUP

    def kernel(place_ref, *refs):
        sources = refs[:4] if len(arrays) == 4 else [refs[0].at[a] for a in range(4)]
        out_ref, got, cut, in_sem, out_sem = refs[-5:]

        def load(g, a):
            return pltpu.make_async_copy(
                sources[a].at[0:HALF, pl.ds(g * GROUP * HD, GROUP * HD)], got.at[g, a], in_sem.at[g, a]
            )

        def store(g):
            at = pl.ds(place_ref[0] * WIDE + g * GROUP, GROUP)
            return pltpu.make_async_copy(cut.at[pl.ds(g * GROUP, GROUP)], out_ref.at[at], out_sem.at[g])

        for g in range(groups):
            for a in range(4):
                load(g, a).start()
        for g in range(groups):
            for a in range(4):
                load(g, a).wait()
                for h in range(GROUP):
                    cut[g * GROUP + h, a] = got[g, a, :, h * HD : (h + 1) * HD]
            store(g).start()
        for g in range(groups):
            store(g).wait()

    extra = [] if whole is None else [whole]
    return call(
        kernel, "spread_heads",
        jax.ShapeDtypeStruct((2 * WIDE, 4, HALF, HD), BF), 1, len(arrays) + len(extra),
        [
            pltpu.VMEM((groups, 4, HALF, GROUP * HD), BF),
            pltpu.VMEM((heads, 4, HALF, HD), BF),
            pltpu.SemaphoreType.DMA((groups, 4)),
            pltpu.SemaphoreType.DMA((groups,)),
        ],
        50 if extra else 56, 4 << 20, aliases={1 + len(arrays): 0} if extra else None,
    )(base[None], *arrays, *extra)


def attend_kernel(
    place_ref, picks_ref, own_hbm, other_hbm,
    first_hbm, mine_hbm, theirs_hbm,
    own_ref, other_ref, kt_ref, vt_ref, s0_ref, s1_ref, t0_ref, t1_ref, d_ref, low_ref, ds_ref,
    mine_ref, sum_ref, theirs_ref, first_ref, in_sem, first_sem, mine_sem, theirs_sem,
):
    nb = picks_ref.shape[0]
    half_at, seg = place_ref[0], place_ref[1]
    scale = 1.0 / math.sqrt(HD)
    power = scale * math.log2(math.e)
    s_refs, t_refs = (s0_ref, s1_ref), (t0_ref, t1_ref)
    chunks = [(j, half) for half in range(2) for j in range(TOPK + 1)]
    rows = [pl.ds(n * ROWS, ROWS) for n in range(len(chunks))]

    edges = (0, 1, 3, 9, nb)

    def loads(k):
        at = pl.ds(edges[k] * PART, (edges[k + 1] - edges[k]) * PART)
        return (
            pltpu.make_async_copy(own_hbm.at[at], own_ref.at[at], in_sem.at[k, 0]),
            pltpu.make_async_copy(other_hbm.at[at], other_ref.at[at], in_sem.at[k, 1]),
        )

    def arrive(k):
        for copy in loads(k):
            copy.wait()

    def part(a, half, b):
        ref = own_ref if half == 0 else other_ref
        return ref[pl.ds(b * PART, PART), a].reshape(ROWS, HD)

    def slots_of(i):
        return [picks_ref[i, j] for j in range(TOPK)] + [i]

    def turn(b):
        for half in range(2):
            kt_ref[half * nb + b] = part(0, half, b).T
            vt_ref[half * nb + b] = part(1, half, b).T

    def scores(i, buf):
        qt = part(2, 0, i).T
        slots = slots_of(i)
        key_at = lax.broadcasted_iota(jnp.int32, (ROWS, ROWS), 0)
        query_at = lax.broadcasted_iota(jnp.int32, (ROWS, ROWS), 1)
        top = jnp.full((8, ROWS), -jnp.inf, F32)
        for n, (j, half) in enumerate(chunks):
            s = dot(part(0, half, slots[j]), qt)
            if j < TOPK:
                valid = slots[j] < i
            elif half == 0:
                valid = key_at <= query_at
            else:
                valid = key_at // HALF < query_at // HALF + half_at
            s = jnp.where(valid, s, -jnp.inf)
            s_refs[buf][rows[n]] = s
            top = jnp.maximum(top, jnp.max(s.reshape(ROWS // 8, 8, ROWS), axis=0))
        t_refs[buf][...] = jnp.broadcast_to(jnp.max(top, axis=0, keepdims=True), (8, ROWS))

    def add_terms(a, terms, slots):
        for n, (j, half) in enumerate(chunks):
            acc = mine_ref if half == 0 else sum_ref
            at = pl.ds(slots[j] * PART, PART)
            term = terms[n * ROWS : (n + 1) * ROWS].reshape(PART, HALF, HD)
            if j < TOPK:
                acc[a, at] += term
            else:
                acc[a, at] = term

    def flat(ref, slots):
        return jnp.concatenate([ref[half * nb + slots[j]] for j, half in chunks], axis=1)

    def rest(i, buf):
        s_ref = s_refs[buf]
        q, g = part(2, 0, i), part(3, 0, i)
        gt = g.T
        slots = slots_of(i)
        top = t_refs[buf][...]
        total = jnp.zeros((8, ROWS), F32)
        for n in range(len(chunks)):
            e = jnp.exp2((s_ref[rows[n]].reshape(ROWS // 8, 8, ROWS) - top) * power)
            s_ref[rows[n]] = e.reshape(ROWS, ROWS)
            total = total + jnp.sum(e, axis=0)
        t_refs[buf][...] = jnp.broadcast_to(1.0 / jnp.sum(total, axis=0, keepdims=True), (8, ROWS))
        inverse = t_refs[buf][...]
        for n in range(len(chunks)):
            low = s_ref[rows[n]].reshape(ROWS // 8, 8, ROWS) * inverse
            low_ref[rows[n]] = low.reshape(ROWS, ROWS).astype(BF)
        out_t = dot(flat(vt_ref, slots), low_ref[...])
        add_terms(1, dot(low_ref[...], g), slots)
        out = out_t.astype(BF).T
        delta = jnp.sum(gt.astype(F32) * out_t.astype(BF).astype(F32), axis=0, keepdims=True)
        d_ref[...] = jnp.broadcast_to(delta, (8, ROWS))
        delta = d_ref[...]
        for n, (j, half) in enumerate(chunks):
            dp = dot(part(1, half, slots[j]), gt).reshape(ROWS // 8, 8, ROWS)
            ds = s_ref[rows[n]].reshape(ROWS // 8, 8, ROWS) * inverse * (dp - delta)
            ds_ref[rows[n]] = ds.reshape(ROWS, ROWS).astype(BF)
        query_t = dot(flat(kt_ref, slots), ds_ref[...])
        add_terms(0, dot(ds_ref[...], q), slots)
        query = (query_t * scale).astype(BF).T
        first = jnp.where(seg == 0, out.astype(F32), query.astype(F32)).astype(BF)
        first_ref[pl.ds(i * PART, PART)] = first.reshape(PART, HALF, HD)

    def send_first(p):
        at = pl.ds(p * 2 * PART, 2 * PART)
        return pltpu.make_async_copy(first_ref.at[at], first_hbm.at[at, 0], first_sem.at[p])

    for k in range(len(edges) - 1):
        for copy in loads(k):
            copy.start()
    arrive(0)
    turn(0)
    scores(0, 0)

    def pair(p, carry):
        i = 2 * p
        later = jnp.minimum(i + 2, nb - 1)

        for k in range(1, len(edges) - 1):

            @pl.when(i + 1 == edges[k])
            def _(k=k):
                arrive(k)

        turn(i + 1)
        turn(later)
        scores(i + 1, 1)
        rest(i, 0)
        scores(later, 0)
        rest(i + 1, 1)
        send_first(p).start()
        return carry

    lax.fori_loop(0, nb // 2, pair, 0)

    def send_mine(a):
        return pltpu.make_async_copy(mine_ref.at[a], mine_hbm.at[a], mine_sem.at[a])

    def send_theirs(b):
        at = pl.ds(b * 4 * PART, 4 * PART)
        return pltpu.make_async_copy(theirs_ref.at[:, at], theirs_hbm.at[:, at], theirs_sem.at[b])

    for a in range(2):
        send_mine(a).start()
    for b in range(nb // 4):
        at = pl.ds(b * 4 * PART, 4 * PART)
        for a in range(2):
            theirs_ref[a, at] = sum_ref[a, at].astype(BF)
        send_theirs(b).start()
    for p in range(nb // 2):
        send_first(p).wait()
    for a in range(2):
        send_mine(a).wait()
    for b in range(nb // 4):
        send_theirs(b).wait()


def attend(place, picks, own, other):
    nb = picks.shape[0]
    n = nb * PART
    work = 6 * 2 * nb * ROWS * KEYS * HD
    return call(
        attend_kernel, "attend_head",
        [
            jax.ShapeDtypeStruct((n, 3, HALF, HD), BF),
            jax.ShapeDtypeStruct((2, n, HALF, HD), F32),
            jax.ShapeDtypeStruct((2, n, HALF, HD), BF),
        ],
        2, 2,
        [
            pltpu.VMEM((n, 4, HALF, HD), BF),
            pltpu.VMEM((n, 2, HALF, HD), BF),
            pltpu.VMEM((2 * nb, HD, ROWS), BF),
            pltpu.VMEM((2 * nb, HD, ROWS), BF),
            pltpu.VMEM((KEYS, ROWS), F32),
            pltpu.VMEM((KEYS, ROWS), F32),
            pltpu.VMEM((8, ROWS), F32),
            pltpu.VMEM((8, ROWS), F32),
            pltpu.VMEM((8, ROWS), F32),
            pltpu.VMEM((KEYS, ROWS), BF),
            pltpu.VMEM((KEYS, ROWS), BF),
            pltpu.VMEM((2, n, HALF, HD), F32),
            pltpu.VMEM((2, n, HALF, HD), F32),
            pltpu.VMEM((2, n, HALF, HD), BF),
            pltpu.VMEM((n, HALF, HD), BF),
            pltpu.SemaphoreType.DMA((4, 2)),
            pltpu.SemaphoreType.DMA((nb // 2,)),
            pltpu.SemaphoreType.DMA((2,)),
            pltpu.SemaphoreType.DMA((nb // 4,)),
        ],
        42, 16 << 20, work,
    )(place, picks, own, other)


def combine(whole, mine, got):
    n = whole.shape[0]
    groups = 4
    size = n // groups

    def kernel(whole_ref, mine_hbm, got_hbm, out_hbm, mine_ref, got_ref, out_ref, in_sem, out_sem):
        scale = 1.0 / math.sqrt(HD)
        at = [pl.ds(g * size, size) for g in range(groups)]

        def loads(g):
            return (
                pltpu.make_async_copy(mine_hbm.at[:, at[g]], mine_ref.at[:, at[g]], in_sem.at[g, 0]),
                pltpu.make_async_copy(got_hbm.at[:, at[g]], got_ref.at[:, at[g]], in_sem.at[g, 1]),
            )

        def store(g):
            return pltpu.make_async_copy(out_ref.at[at[g]], out_hbm.at[at[g], 1:3], out_sem.at[g])

        for g in range(groups):
            for copy in loads(g):
                copy.start()
        for g in range(groups):
            for copy in loads(g):
                copy.wait()
            for a in range(2):
                value = mine_ref[a, at[g]] + got_ref[a, at[g]].astype(F32)
                out_ref[at[g], a] = (value * scale if a == 0 else value).astype(BF)
            store(g).start()
        for g in range(groups):
            store(g).wait()

    return call(
        kernel, "combine_halves", jax.ShapeDtypeStruct(whole.shape, BF), 0, 3,
        [
            pltpu.VMEM((2, n, HALF, HD), F32),
            pltpu.VMEM((2, n, HALF, HD), BF),
            pltpu.VMEM((n, 2, HALF, HD), BF),
            pltpu.SemaphoreType.DMA((groups, 2)),
            pltpu.SemaphoreType.DMA((groups,)),
        ],
        12, 8 << 20, aliases={0: 0},
    )(whole, mine, got)


def gather(core, source, base, high, results=None):
    heads = 4 * GROUP
    size = 4
    groups = heads // size
    rows = slice(HALF, 2 * HALF) if high else slice(0, HALF)

    def kernel(place_ref, source_ref, *refs):
        outs = refs[-8:-4]
        got, cut, in_sem, out_sem = refs[-4:]

        def load(g):
            at = pl.ds(place_ref[1] + g * size, size)
            return pltpu.make_async_copy(source_ref.at[at], got.at[g], in_sem.at[g])

        def store(g, a):
            cols = pl.ds(g * size * HD, size * HD)
            return pltpu.make_async_copy(cut.at[g, a], outs[a].at[0, rows, cols], out_sem.at[g, a])

        for g in range(groups):
            load(g).start()
        for g in range(groups):
            load(g).wait()
            for a in range(4):
                live = place_ref[0] == (1 if a == 0 else 0)
                for h in range(size):
                    value = got[g, h, max(a - 1, 0)]
                    cut[g, a, :, h * HD : (h + 1) * HD] = jnp.where(live, value, jnp.zeros_like(value))
                store(g, a).start()
        for g in range(groups):
            for a in range(4):
                store(g, a).wait()

    extra = [] if results is None else list(results)
    return call(
        kernel, "gather_heads", [jax.ShapeDtypeStruct((1, 2 * HALF, heads * HD), BF)] * 4, 1, 1 + len(extra),
        [
            pltpu.VMEM((groups, size, 3, HALF, HD), BF),
            pltpu.VMEM((groups, 4, HALF, size * HD), BF),
            pltpu.SemaphoreType.DMA((groups,)),
            pltpu.SemaphoreType.DMA((groups, 4)),
        ],
        8, 4 << 20, aliases={2 + a: a for a in range(4)} if extra else None,
    )(jnp.stack([core, base]), source, *extra)


def cut_out(name, out_shape, vmem, pieces, place, *sources, direct=False):
    def kernel(place_ref, *refs):
        out_ref, held, in_sem, out_sem = refs[-4:]
        first, then = [], []
        for n, (src, at) in enumerate(pieces(place_ref, refs[:-4])):
            if direct:
                first.append(pltpu.make_async_copy(src, out_ref.at[at], in_sem.at[n]))
            else:
                first.append(pltpu.make_async_copy(src, held.at[at], in_sem.at[n]))
                then.append(pltpu.make_async_copy(held.at[at], out_ref.at[at], out_sem.at[n]))
        for copy in first:
            copy.start()
        for n, copy in enumerate(first):
            copy.wait()
            if not direct:
                then[n].start()
        for copy in then:
            copy.wait()

    return call(
        kernel, name, jax.ShapeDtypeStruct(out_shape, BF), 1, len(sources),
        [pltpu.VMEM((8, HD) if direct else out_shape, BF), pltpu.SemaphoreType.DMA((4,)), pltpu.SemaphoreType.DMA((4,))],
        vmem, 2 << 20,
    )(place[None], *sources)


CHIPS = ("ctx", "tp")
SWAP = [(0, 1), (1, 0)]


def on_device(queries, keys, values, out_grad, chosen):
    heads = queries.shape[2] // HD
    core = lax.axis_index("pipe").astype(jnp.int32)
    seg = (lax.axis_index(CHIPS) // WIDE).astype(jnp.int32)

    place = jnp.stack([core ^ seg, seg])
    arrays = (keys, values, queries, out_grad)
    theirs = cut_out(
        "cut_tokens", (4, HALF, heads * HD), 56,
        lambda _, refs: [(ref.at[0, HALF : 2 * HALF], a) for a, ref in enumerate(refs)],
        core, *arrays,
    )
    got = lax.ppermute(theirs, "pipe", SWAP)
    other_chosen = lax.ppermute(chosen, "pipe", SWAP)
    parts = spread(core, [x[0] for x in arrays], core)
    parts = spread(core, [got], 1 - core, parts)
    parts, other_chosen = lax.optimization_barrier((parts, other_chosen))

    own = lax.all_to_all(parts, CHIPS, 0, 0, tiled=True)
    own, other_chosen = lax.optimization_barrier((own, other_chosen))
    picks = jnp.where(seg == core, chosen, other_chosen)[0]
    n = own.shape[0]
    mine = cut_out(
        "cut_keys", (n, 2, HALF, HD), 50,
        lambda _, refs: [
            (refs[0].at[pl.ds(g * n // 4, n // 4), 0:2], pl.ds(g * n // 4, n // 4)) for g in range(4)
        ],
        core, own,
    )
    other = lax.ppermute(mine, "pipe", SWAP)
    first, mine, theirs = attend(place, picks, own, other)
    whole = combine(first, mine, lax.ppermute(theirs, "pipe", SWAP))

    back = lax.all_to_all(whole, CHIPS, 0, 0, tiled=True)
    theirs = cut_out(
        "cut_heads", (heads, 3, HALF, HD), 4,
        lambda place_ref, refs: [
            (refs[0].at[pl.ds(place_ref[0] * WIDE + g * GROUP, GROUP)], pl.ds(g * GROUP, GROUP)) for g in range(4)
        ],
        core, back, direct=True,
    )
    got = lax.ppermute(theirs, "pipe", SWAP)
    results = gather(core, back, (1 - core) * WIDE, True)
    return tuple(gather(core, got, core * 0, False, results))


def solution(mesh):
    placed = P("pipe", CHIPS, None)
    return jax.shard_map(
        on_device,
        mesh=mesh,
        in_specs=(placed,) * 4 + (P("pipe", None, None),),
        out_specs=(placed,) * 4,
        check_vma=False,
    )
```
